32 devices in a mesh: tile: 8 (over z, y), seg: 4 (over x, core).
Axes of the slice: x: 2, y: 2, z: 4, core: 2. Of those that a mesh axis runs over, the one named last changes fastest.
Arguments:
- patches: bfloat16 [8, 257, 1536], P('tile'), may hold values from -6 to 6
- vit_norm_gain: float32 [1536], replicated, may hold values from 0.5 to 1.5
- vit_query: bfloat16 [1536, 1536], P('tile', 'seg'), may hold values from -1 to 1
- vit_key: bfloat16 [1536, 1536], P('tile', 'seg'), may hold values from -1 to 1
- vit_value: bfloat16 [1536, 1536], P('tile', 'seg'), may hold values from -0.15625 to 0.15625
- vit_out: bfloat16 [1536, 1536], P('seg'), may hold values from -0.15625 to 0.15625
- layer_scale: float32 [1536], replicated, may hold values from 0.25 to 2.5
- final_gain: float32 [1536], replicated, may hold values from 0.5 to 1.5
- embed_proj: bfloat16 [1536, 768], P(None, 'seg'), may hold values from -0.15625 to 0.15625
- embed_bias: float32 [768], P('seg'), may hold values from -3 to 3
- slide_pos: int32 [8], replicated, may hold values from 0 to 2047, as said below
- cached: bfloat16 [2048, 768], P('tile'), may hold values from -6 to 6
- kept: int32 [2048], P('tile'), may hold values 0 or 1
- mask_token: float32 [768], replicated, may hold values from -4 to 4
- slide_gain: float32 [768], replicated, may hold values from 0.5 to 1.5
- slide_query: bfloat16 [768, 768], P(None, 'seg'), may hold values from -1 to 1
- slide_key: bfloat16 [768, 768], P(None, 'seg'), may hold values from -1 to 1
- slide_value: bfloat16 [768, 768], P(None, 'seg'), may hold values from -0.21875 to 0.21875
- slide_out: bfloat16 [768, 768], P('seg'), may hold values from -0.21875 to 0.21875
- offsets: int32 [5, 12], replicated, may hold values from 0 to 15, as said below
Outputs:
- slide_next: bfloat16 [2048, 768], P(('tile', 'seg'))
The draws below stay inside these ranges and needn't reach their ends.
Inputs may be any that keep to these rules, and one draw needn't show every extreme that they name: `slide_pos`: distinct positions of the slide sequence. `offsets`: entry [b, h] is below 2 ** b.
All inputs are finite; a program needn't handle non-finite values. No bound on the sum of `kept` on one device may be relied on, other than what follows from the above.
Results may differ from the reference program's by a relative error of at most 0.0095.
Values may be sent and summed in bfloat16 or wider, within the bound.
No kernel may reach another device: no remote copies, remote signals or barrier semaphores. Data moves between devices by JAX's collectives and lax.ppermute only.
A program may use at most 64 MiB of HBM per device.

```python
import math
import jax
import jax.numpy as jnp
from jax import lax

DV = 1536
HV = 24
DS = 768
HS = 12
TOKT = 257
LDEV = 256
NBR = 5
NEWTOT = 8
SEQ = 2048


def drawn_weight(key, row_count, col_count):
    return jnp.clip(jax.random.normal(key, (row_count, col_count), jnp.float32), -3.0, 3.0) / math.sqrt(row_count)


def draw_vit_query(key, part):
    key = jax.random.fold_in(key, 11)
    return drawn_weight(key, DV, DV).astype(jnp.bfloat16)


def draw_vit_key(key, part):
    key = jax.random.fold_in(key, 12)
    return drawn_weight(key, DV, DV).astype(jnp.bfloat16)


def draw_slide_query(key, part):
    key = jax.random.fold_in(key, 13)
    return drawn_weight(key, DS, DS).astype(jnp.bfloat16)


def draw_slide_key(key, part):
    key = jax.random.fold_in(key, 14)
    return drawn_weight(key, DS, DS).astype(jnp.bfloat16)


def draw_patches(key, part):
    key = jax.random.fold_in(key, 15)
    return jnp.clip(jax.random.normal(key, (NEWTOT, TOKT, DV), jnp.float32), -6.0, 6.0).astype(jnp.bfloat16)


def draw_cached(key, part):
    key = jax.random.fold_in(key, 16)
    pattern = jnp.clip(jax.random.normal(jax.random.fold_in(key, 5), (16, DS), jnp.float32), -3.0, 3.0) * 0.8
    periodic = jnp.tile(pattern, (SEQ // 16, 1))
    return jnp.clip(jax.random.normal(key, (SEQ, DS), jnp.float32) + periodic, -6.0, 6.0).astype(jnp.bfloat16)


def draw_slide_pos(key, part):
    key = jax.random.fold_in(key, 17)
    order = jax.random.permutation(key, SEQ).astype(jnp.int32)
    first_value = order[0]
    order = jnp.where(order == 0, first_value, jnp.where(order == first_value, 0, order))
    second_value = order[1]
    order = jnp.where(order == SEQ - 1, second_value, jnp.where(order == second_value, SEQ - 1, order))
    chosen = order[:NEWTOT]
    shuffle = jax.random.permutation(jax.random.fold_in(key, 2), NEWTOT)
    return chosen[shuffle].astype(jnp.int32)


def draw_offsets(key, part):
    key = jax.random.fold_in(key, 18)
    strides = (2 ** jnp.arange(NBR, dtype=jnp.int32))[:, None]
    raw_values = jax.random.randint(key, (NBR, HS), 0, 1 << 20, jnp.int32)
    residues = raw_values % strides
    pick_head = jax.random.randint(jax.random.fold_in(key, 1), (NBR, 1), 0, HS, jnp.int32)
    head_ids = jnp.arange(HS, dtype=jnp.int32)[None, :]
    return jnp.where(head_ids == pick_head, strides - 1, residues).astype(jnp.int32)


def plant(values, own_key, smallest, largest):
    place = [jax.random.randint(jax.random.fold_in(own_key, axis), (), 0, length) for axis, length in enumerate(values.shape)]
    widest = values.shape.index(max(values.shape))
    beside = place[:widest] + [(place[widest] + 1) % values.shape[widest]] + place[widest + 1:]
    return values.at[tuple(place)].set(smallest).at[tuple(beside)].set(largest)


def block_levels(own_key, shape, pieces, smallest, top_value):
    def one(dim, parts):
        steps = jax.random.uniform(jax.random.fold_in(jax.random.fold_in(own_key, 6), dim), (parts,), jnp.float32, smallest / len(pieces), top_value / len(pieces))
        return jnp.repeat(jnp.exp(steps), shape[dim] // parts).reshape((-1,) + (1,) * (len(shape) - dim - 1))

    factor_of = one(*pieces[0])
    for cut in pieces[1:]:
        factor_of = factor_of * one(*cut)
    return factor_of


def normal_values(rng, dims, scale, most, shards=(), held_as=jnp.bfloat16):
    loudness = block_levels(rng, dims, shards, -0.22, 0.18) if shards else 1.0
    values = jax.random.normal(rng, dims, jnp.float32) * scale * loudness
    return jnp.minimum(jnp.maximum(values, -most), most).astype(held_as)


def setup_inputs(seed: int = 0) -> dict:
    key_of = jax.random.split(jax.random.key(seed), 21)
    patches = draw_patches(jax.random.fold_in(key_of[20], 71), 0)
    vit_norm_gain = jnp.clip(1.0 + 0.1 * jax.random.normal(key_of[1], (DV,), jnp.float32), 0.5, 1.5)
    vit_query = draw_vit_query(jax.random.fold_in(key_of[20], 71), 0)
    vit_key = draw_vit_key(jax.random.fold_in(key_of[20], 71), 0)
    vit_value = normal_values(key_of[4], (DV, DV), DV ** -0.5, 0.15625, ((0, 8), (1, 4)))
    vit_out = normal_values(key_of[5], (DV, DV), DV ** -0.5, 0.15625, ((0, 4),))
    layer_scale = jnp.clip(jnp.exp(jax.random.uniform(key_of[6], (DV,), jnp.float32, math.log(0.25), math.log(2.5))), 0.25, 2.5)
    final_gain = jnp.clip(1.0 + 0.1 * jax.random.normal(key_of[7], (DV,), jnp.float32), 0.5, 1.5)
    embed_proj = normal_values(key_of[8], (DV, DS), DV ** -0.5, 0.15625, ((1, 4),))
    embed_bias = normal_values(key_of[9], (DS,), 0.5, 3.0, ((0, 4),), jnp.float32)
    slide_pos = draw_slide_pos(jax.random.fold_in(key_of[20], 71), 0)
    cached = draw_cached(jax.random.fold_in(key_of[20], 71), 0)
    kept = plant((jax.random.randint(key_of[12], (SEQ,), 0, 4) < 3).astype(jnp.int32), jax.random.fold_in(key_of[12], 1), 0, 1)
    mask_token = normal_values(key_of[13], (DS,), 1.0, 4.0, (), jnp.float32)
    slide_gain = jnp.clip(1.0 + 0.1 * jax.random.normal(key_of[14], (DS,), jnp.float32), 0.5, 1.5)
    slide_query = draw_slide_query(jax.random.fold_in(key_of[20], 71), 0)
    slide_key = draw_slide_key(jax.random.fold_in(key_of[20], 71), 0)
    slide_value = normal_values(key_of[17], (DS, DS), DS ** -0.5, 0.21875, ((1, 4),))
    slide_out = normal_values(key_of[18], (DS, DS), DS ** -0.5, 0.21875, ((0, 4),))
    offsets = draw_offsets(jax.random.fold_in(key_of[20], 71), 0)
    return {"patches": patches, "vit_norm_gain": vit_norm_gain, "vit_query": vit_query, "vit_key": vit_key, "vit_value": vit_value, "vit_out": vit_out, "layer_scale": layer_scale, "final_gain": final_gain, "embed_proj": embed_proj, "embed_bias": embed_bias, "slide_pos": slide_pos, "cached": cached, "kept": kept, "mask_token": mask_token, "slide_gain": slide_gain, "slide_query": slide_query, "slide_key": slide_key, "slide_value": slide_value, "slide_out": slide_out, "offsets": offsets}


epsilon = 1e-06

def layer_norm(values, scaling):
    center = values - lax.optimization_barrier(jnp.mean(values, axis=-1, keepdims=True))
    spread = lax.optimization_barrier(jnp.mean(center * center, axis=-1, keepdims=True))
    return center * lax.rsqrt(spread + epsilon) * scaling

def as_float(values):
    return lax.optimization_barrier(values).astype(jnp.float32)

def reference(patches, vit_norm_gain, vit_query, vit_key, vit_value, vit_out, layer_scale, final_gain, embed_proj, embed_bias, slide_pos, cached, kept, mask_token, slide_gain, slide_query, slide_key, slide_value, slide_out, offsets):
    head_size = DV // HV
    scale_vit = 1.0 / math.sqrt(head_size)

    def encode(tile_tokens):
        normed = layer_norm(tile_tokens.astype(jnp.float32), vit_norm_gain).astype(jnp.bfloat16)

        def heads_of(rows, matrix):
            result = jnp.dot(rows, matrix, preferred_element_type=jnp.float32).astype(jnp.bfloat16)
            return as_float(result.reshape(rows.shape[0], HV, head_size))
        queries = heads_of(normed[0:1], vit_query)[0]
        keys_vit = heads_of(normed, vit_key)
        values_vit = heads_of(normed, vit_value)
        scores = jnp.einsum('hd,khd->hk', queries, keys_vit) * scale_vit
        highest = lax.optimization_barrier(jnp.max(scores, axis=-1, keepdims=True))
        exponent = jnp.exp(scores - highest)
        weights_vit = (exponent / lax.optimization_barrier(jnp.sum(exponent, axis=-1, keepdims=True))).astype(jnp.bfloat16)
        mixture = jnp.einsum('hk,khd->hd', as_float(weights_vit), values_vit).reshape(DV).astype(jnp.bfloat16)
        return (mixture, tile_tokens[0].astype(jnp.float32))
    class_mix, class_token = lax.map(encode, patches)
    attended = jnp.dot(class_mix, vit_out, preferred_element_type=jnp.float32)
    pooled = class_token + layer_scale * attended
    summary = layer_norm(pooled, final_gain).astype(jnp.bfloat16)
    embedded = (jnp.dot(summary, embed_proj, preferred_element_type=jnp.float32) + embed_bias).astype(jnp.bfloat16)
    arrived = jnp.zeros((SEQ,), jnp.int32).at[slide_pos].set(1)
    placed = jnp.zeros((SEQ, DS), jnp.bfloat16).at[slide_pos].set(embedded)
    mask_row = mask_token.astype(jnp.bfloat16)
    slide_rows = jnp.where(kept[:, None] == 0, mask_row[None, :], jnp.where(arrived[:, None] == 1, placed, cached))
    slide_normed = layer_norm(slide_rows.astype(jnp.float32), slide_gain).astype(jnp.bfloat16)
    slide_q = jnp.dot(slide_normed, slide_query, preferred_element_type=jnp.float32).astype(jnp.bfloat16)
    slide_k = jnp.dot(slide_normed, slide_key, preferred_element_type=jnp.float32).astype(jnp.bfloat16)
    slide_v = jnp.dot(slide_normed, slide_value, preferred_element_type=jnp.float32).astype(jnp.bfloat16)
    head_dim = DS // HS
    scale_slide = 1.0 / math.sqrt(head_dim)
    head_results = []
    for head in range(HS):
        query_head = slide_q[:, head * head_dim:(head + 1) * head_dim]
        key_head = slide_k[:, head * head_dim:(head + 1) * head_dim]
        value_head = slide_v[:, head * head_dim:(head + 1) * head_dim]
        for branch in range(NBR):
            stride = 2 ** branch
            residue = offsets[branch, head]
            segment_keys = min(2 * LDEV * 4 ** branch, SEQ) // stride

            def select(values):
                shaped = values.reshape(SEQ // stride, stride, head_dim)
                picked = lax.dynamic_index_in_dim(shaped, residue, 1, keepdims=False)
                return as_float(picked.reshape(-1, segment_keys, head_dim))

            def expand(values, filler):
                shaped = jnp.full((SEQ // stride, stride) + values.shape[1:], filler, jnp.float32)
                placed_rows = lax.dynamic_update_slice_in_dim(shaped, values[:, None], residue, 1)
                return placed_rows.reshape((SEQ,) + values.shape[1:])
            scores_seg = jnp.einsum('sqd,skd->sqk', select(query_head), select(key_head)) * scale_slide
            highest_seg = lax.optimization_barrier(jnp.max(scores_seg, axis=-1))
            exponent_seg = jnp.exp(scores_seg - highest_seg[..., None])
            denom_seg = lax.optimization_barrier(jnp.sum(exponent_seg, axis=-1))
            numer_seg = jnp.einsum('sqk,skd->sqd', as_float(exponent_seg.astype(jnp.bfloat16)), select(value_head))
            highest_seg = highest_seg.reshape(-1)
            denom_seg = denom_seg.reshape(-1)
            numer_seg = numer_seg.reshape(-1, head_dim)
            if branch == 0:
                run_max, run_den, run_num = (highest_seg, denom_seg, numer_seg)
            else:
                full_max = expand(highest_seg, -1e+30)
                full_den = expand(denom_seg, 0.0)
                full_num = expand(numer_seg, 0.0)
                new_max = jnp.maximum(run_max, full_max)
                keep_old = jnp.exp(run_max - new_max)
                take_new = jnp.exp(full_max - new_max)
                run_den = run_den * keep_old + full_den * take_new
                run_num = run_num * keep_old[:, None] + full_num * take_new[:, None]
                run_max = new_max
        head_results.append(run_num / run_den[:, None])
    attended_slide = jnp.concatenate(head_results, axis=1).astype(jnp.bfloat16)
    update = jnp.dot(attended_slide, slide_out, preferred_element_type=jnp.float32)
    return (slide_rows.astype(jnp.float32) + update).astype(jnp.bfloat16)
```

```python
import functools
import math

import jax
import jax.numpy as jnp
from jax import lax
from jax.experimental import pallas as pl
from jax.experimental.pallas import tpu as pltpu
from jax.sharding import PartitionSpec as P

DV = 1536
HV = 24
DS = 768
HS = 12
HEAD = 64

EPS = 1e-06
LOW = -1e30
F32 = jnp.float32
BF16 = jnp.bfloat16
I32 = jnp.int32
VMEM = pl.BlockSpec(memory_space=pltpu.VMEM)
SMEM = pl.BlockSpec(memory_space=pltpu.SMEM)
NT = (((1,), (1,)), ((), ()))
ROOM = 56 * 1024 * 1024


def params():
    return pltpu.CompilerParams(vmem_limit_bytes=ROOM)


def round_up(value, unit):
    return -(-value // unit) * unit


def layer_norm(values, scaling):
    center = values - jnp.mean(values, axis=-1, keepdims=True)
    spread = jnp.mean(center * center, axis=-1, keepdims=True)
    return center * lax.rsqrt(spread + EPS) * scaling


def dot(a, b):
    return jnp.dot(a, b, preferred_element_type=F32)


def dot_nt(a, b):
    return lax.dot_general(a, b, NT, preferred_element_type=F32)


def class_kernel(fresh, patch_ref, gain_ref, pos_ref, kept_ref, where_ref, pack_ref):
    parts, width = pack_ref.shape
    cut = DV // parts
    rows = kept_ref.shape[0]
    row = patch_ref[0, 0:1].astype(F32)
    normed = layer_norm(row, gain_ref[...]).astype(BF16).astype(F32)
    first = where_ref[0] * rows
    ids = lax.broadcasted_iota(I32, (rows, width), 0) + first
    hit = (ids == pos_ref[...]) & (kept_ref[...] != 0)
    flags = jnp.max(jnp.where(hit, 1.0, 0.0), axis=0, keepdims=True)
    pack_ref[...] = jnp.broadcast_to(flags, (parts, width))
    for part in range(parts):
        pack_ref[part : part + 1, 0:cut] = normed[:, part * cut : (part + 1) * cut]


def base_kernel(
    cached_ref, kept_ref, mask_ref, gain_ref, wq_ref, wk_ref, wv_ref, rows_ref, q_ref, kv_ref
):
    rows = jnp.where(
        kept_ref[...] == 0, mask_ref[...].astype(BF16).astype(F32), cached_ref[...].astype(F32)
    )
    rows_ref[...] = rows.astype(BF16)
    normed = layer_norm(rows, gain_ref[...]).astype(BF16)
    project(normed, wq_ref, wk_ref, wv_ref, q_ref, kv_ref)


def project(normed, wq_ref, wk_ref, wv_ref, q_ref, kv_ref):
    q = dot(normed, wq_ref[...]).astype(BF16) * BF16(1.0 / math.sqrt(HEAD))
    k = dot(normed, wk_ref[...]).astype(BF16)
    v = dot(normed, wv_ref[...]).astype(BF16)
    q_ref[:, 0:192] = q
    q_ref[:, 192:256] = jnp.zeros((q.shape[0], 64), BF16)
    kv_ref[:, 0:192] = k
    kv_ref[:, 192:256] = v[:, 128:192]
    kv_ref[:, 256:384] = v[:, 0:128]


def query_kernel(cut, pack_ref, wq_ref, part_ref):
    rows = pack_ref[:, 0:cut].astype(BF16)
    part = dot(rows, wq_ref[...])
    if len(part_ref.shape) == 3:
        part_ref[...] = jnp.broadcast_to(part[None], part_ref.shape)
    else:
        part_ref[...] = part


def fold_kernel(part_ref, wk_ref, fold_ref):
    if len(part_ref.shape) == 3:
        queries = part_ref[0]
        for index in range(1, part_ref.shape[0]):
            queries = queries + part_ref[index]
    else:
        queries = part_ref[...]
    tiles, width = queries.shape
    queries = queries.astype(BF16).astype(F32)
    spread = jnp.broadcast_to(queries[:, None], (tiles, 8, width))
    head = lax.broadcasted_iota(I32, spread.shape, 1)
    lane = lax.broadcasted_iota(I32, spread.shape, 2)
    spread = jnp.where(lane // HEAD == head, spread, 0.0).reshape(tiles * 8, width).astype(BF16)
    cut = wk_ref.shape[0]
    result = dot_nt(spread, wk_ref[...]).reshape(tiles, 8, cut)
    fold_ref[:, :, 0:cut] = result


def tile_kernel(
    cut, patch_ref, gain_ref, fold_ref, wv_ref, wo_ref, scale_ref, bias_ref, where_ref,
    sent_ref, fold_s,
):
    for part in range(fold_ref.shape[0]):
        fold_s[:, part * cut : (part + 1) * cut] = fold_ref[part, :, 0:cut]
    tokens = patch_ref[0].astype(F32)
    normed = layer_norm(tokens, gain_ref[...]).astype(BF16)
    scores = dot_nt(fold_s[...].astype(BF16), normed) * (1.0 / math.sqrt(HEAD))
    highest = jnp.max(scores, axis=-1, keepdims=True)
    exponent = jnp.exp(scores - highest)
    prob = (exponent / jnp.sum(exponent, axis=-1, keepdims=True)).astype(BF16)
    mixed = dot(prob, normed).astype(BF16)
    values = dot(mixed, wv_ref[...])
    head = lax.broadcasted_iota(I32, values.shape, 0)
    lane = lax.broadcasted_iota(I32, values.shape, 1)
    tmix = jnp.sum(jnp.where(lane // HEAD == head, values, 0.0), axis=0, keepdims=True)
    tmix = jnp.broadcast_to(tmix, (8, tmix.shape[1])).astype(BF16)
    share = dot(tmix, wo_ref[...])[0:1] * scale_ref[...]
    share = share + jnp.where(where_ref[1] == 0, tokens[0:1], 0.0)
    devices = sent_ref.shape[0]
    sent_ref[:, 0:DV] = jnp.broadcast_to(share, (devices, DV))
    sent_ref[:, DV:] = jnp.broadcast_to(bias_ref[...], (devices, bias_ref.shape[1]))


def branch_rows(position, axis, offset_ref, where_ref, head, span, total):
    shape = (1, 8) if axis == 1 else (8, 1)
    branch = lax.broadcasted_iota(I32, shape, axis)
    residue = jnp.full(shape, -1, I32)
    shift = jnp.zeros(shape, I32)
    for b in range(offset_ref.shape[0]):
        residue = jnp.where(branch == b, offset_ref[b, where_ref[1] * 3 + head], residue)
        length = min(2 * span * 4**b, total)
        shift = jnp.where(branch == b, length.bit_length() - 1, shift)
    below = jnp.left_shift(jnp.int32(1), branch) - 1
    mine = jnp.right_shift(jnp.zeros(shape, I32) + where_ref[0] * span, shift)
    return ((position & below) == residue) & (jnp.right_shift(position, shift) == mine)


def value_lanes(head):
    group = {0: 2, 1: 3, 2: 1}[head]
    lane = lax.broadcasted_iota(I32, (1, 256), 1)
    return lane // HEAD == group


def attend(q, q_rows, kv_ref, k_rows, head):
    lane = lax.broadcasted_iota(I32, (1, 256), 1)
    q_head = jnp.where(lane // HEAD == head, q, jnp.zeros_like(q))
    scores = dot_nt(q_head, kv_ref[:, 0:256])
    count = dot(q_rows, k_rows)
    scores = jnp.where(count > 0.5, scores, LOW)
    highest = jnp.max(scores, axis=-1, keepdims=True)
    weight = jnp.exp(scores - highest) * count
    denom = jnp.sum(weight, axis=-1, keepdims=True)
    numer = dot(weight.astype(BF16), kv_ref[:, 128:384])
    return highest, denom, numer


def as_bf16(condition):
    return jnp.where(condition, 1.0, 0.0).astype(BF16)


def merge(old, new):
    old_max, old_den, old_num = old
    new_max, new_den, new_num = new
    top = jnp.maximum(old_max, new_max)
    keep = jnp.exp(old_max - top)
    take = jnp.exp(new_max - top)
    return top, old_den * keep + new_den * take, old_num * keep + new_num * take


def store_state(state, head, ml_ref, acc_ref):
    highest, denom, numer = state
    lane = lax.broadcasted_iota(I32, (1, 128), 1)
    ml = jnp.where(lane == head, highest, ml_ref[...])
    ml_ref[...] = jnp.where(lane == head + 8, denom, ml)
    acc_ref[...] = jnp.where(value_lanes(head), numer, acc_ref[...])


def load_state(head, ml_ref, acc_ref):
    return ml_ref[:, head : head + 1], ml_ref[:, head + 8 : head + 9], acc_ref[...]


def key_rows(step, block, pos_ref, flag_ref, offset_ref, where_ref, head, span, total):
    position = lax.broadcasted_iota(I32, (1, block), 1) + step * block
    rows = branch_rows(position, 0, offset_ref, where_ref, head, span, total)
    taken = (position == pos_ref[...]) & (flag_ref[...] > 0.5)
    taken = jnp.max(jnp.where(taken, 1.0, 0.0), axis=0, keepdims=True)
    return as_bf16(rows & (taken < 0.5))


def base_attention_kernel(
    span, total, q_ref, kv_ref, pos_ref, flag_ref, offset_ref, where_ref, ml_ref, acc_ref
):
    step = pl.program_id(0)
    block = kv_ref.shape[0]
    rows = q_ref.shape[0]

    @pl.when(step == 0)
    def _():
        lane = lax.broadcasted_iota(I32, (rows, 128), 1)
        ml_ref[...] = jnp.where(lane < 8, LOW, 0.0)
        acc_ref[...] = jnp.zeros_like(acc_ref)

    place = lax.broadcasted_iota(I32, (rows, 1), 0) + where_ref[0] * span
    for head in range(3):
        q_rows = as_bf16(branch_rows(place, 1, offset_ref, where_ref, head, span, total))
        k_rows = key_rows(
            step, block, pos_ref, flag_ref, offset_ref, where_ref, head, span, total
        )
        new = attend(q_ref[...], q_rows, kv_ref, k_rows, head)
        store_state(merge(load_state(head, ml_ref, acc_ref), new), head, ml_ref, acc_ref)


def fresh_kernel(
    span, total, shares_ref, final_ref, embed_ref, gain_ref, wq_ref, wk_ref, wv_ref,
    q_ref, kv_ref, pos_ref, posrow_ref, flag_ref, flagrow_ref, ml_ref, acc_ref, rows_ref,
    offset_ref, where_ref, out0_ref, out1_ref, out2_ref, out3_ref, mine_ref,
    fresh_s, qf_s, kvf_s, mlf_s, accf_s, att_s,
):
    step = pl.program_id(0)
    block = kv_ref.shape[0]
    rows = q_ref.shape[0]
    padded = fresh_s.shape[0]
    seg = where_ref[1]

    @pl.when(step == 0)
    def _():
        shares = shares_ref[:, 0:DV]
        groups = shares_ref.shape[0] // 4
        pooled = jnp.sum(shares.reshape(groups, 4, DV), axis=1)
        summary = layer_norm(pooled, final_ref[...]).astype(BF16)
        fresh_s[...] = jnp.zeros_like(fresh_s)
        for part in range(4):
            cols = slice(part * 192, (part + 1) * 192)
            piece = dot(summary, embed_ref[part]) + shares_ref[part : part + 1, DV : DV + 192]
            fresh_s[0:groups, cols] = piece.astype(BF16).astype(F32)
        normed = layer_norm(fresh_s[...], gain_ref[...]).astype(BF16)
        project(normed, wq_ref, wk_ref, wv_ref, qf_s, kvf_s)
        lane = lax.broadcasted_iota(I32, (padded, 128), 1)
        mlf_s[...] = jnp.where(lane < 8, LOW, 0.0)
        accf_s[...] = jnp.zeros_like(accf_s)

    for head in range(3):
        q_rows = as_bf16(branch_rows(pos_ref[...], 1, offset_ref, where_ref, head, span, total))
        k_rows = key_rows(
            step, block, pos_ref, flag_ref, offset_ref, where_ref, head, span, total
        )
        new = attend(qf_s[...], q_rows, kv_ref, k_rows, head)
        store_state(merge(load_state(head, mlf_s, accf_s), new), head, mlf_s, accf_s)

    @pl.when(step == pl.num_programs(0) - 1)
    def _():
        place = lax.broadcasted_iota(I32, (rows, 1), 0) + where_ref[0] * span
        base = jnp.zeros((rows, 256), F32)
        fresh = jnp.zeros((padded, 256), F32)
        for head in range(3):
            q_rows = as_bf16(branch_rows(place, 1, offset_ref, where_ref, head, span, total))
            f_rows = as_bf16(
                branch_rows(pos_ref[...], 1, offset_ref, where_ref, head, span, total)
            )
            k_rows = as_bf16(
                branch_rows(posrow_ref[...], 0, offset_ref, where_ref, head, span, total)
                & (flagrow_ref[...] > 0.5)
            )
            lanes = value_lanes(head)
            new = attend(q_ref[...], q_rows, kvf_s, k_rows, head)
            top, den, num = merge(load_state(head, ml_ref, acc_ref), new)
            base = jnp.where(lanes, num / den, base)
            new = attend(qf_s[...], f_rows, kvf_s, k_rows, head)
            top, den, num = merge(load_state(head, mlf_s, accf_s), new)
            fresh = jnp.where(lanes, num / jnp.where(den > 0.0, den, 1.0), fresh)
        chosen = as_bf16((place == posrow_ref[...]) & (flagrow_ref[...] > 0.5))
        hit = jnp.sum(chosen.astype(F32), axis=1, keepdims=True) > 0.5
        att_s[...] = jnp.where(hit, dot(chosen, fresh.astype(BF16)), base)
        count = rows // 4
        outs = (out0_ref, out1_ref, out2_ref, out3_ref)
        for mask in range(4):
            start = pl.multiple_of((seg ^ mask) * count, count)
            outs[mask][...] = att_s[pl.ds(start, count), :].astype(BF16)
        start = pl.multiple_of(seg * count, count)
        place = lax.broadcasted_iota(I32, (count, 1), 0) + where_ref[0] * span + start
        chosen = as_bf16((place == posrow_ref[...]) & (flagrow_ref[...] > 0.5))
        hit = jnp.sum(chosen.astype(F32), axis=1, keepdims=True) > 0.5
        placed = dot(chosen, fresh_s[...].astype(BF16))
        old = rows_ref[pl.ds(start, count), :].astype(F32)
        mine_ref[...] = jnp.where(hit, placed, old)


def out_kernel(a0_ref, a1_ref, a2_ref, a3_ref, wo_ref, mine_ref, where_ref, out_ref):
    total = mine_ref[...]
    seg = where_ref[1]
    for mask, ref in enumerate((a0_ref, a1_ref, a2_ref, a3_ref)):
        weight = wo_ref[seg ^ mask]
        att = ref[...]
        total = total + dot(att[:, 128:256], weight[0:128])
        total = total + dot(att[:, 64:128], weight[128:192])
    out_ref[...] = total.astype(BF16)


def trade(block, axis, mask):
    count = lax.axis_size(axis)
    return lax.ppermute(block, axis, [(i, i ^ mask) for i in range(count)])


def gather_tile(block):
    return lax.all_gather(block, "tile", axis=0, tiled=True)


def shards(
    patches, vit_norm_gain, vit_query, vit_key, vit_value, vit_out, layer_scale, final_gain,
    embed_proj, embed_bias, slide_pos, cached, kept, mask_token, slide_gain, slide_query,
    slide_key, slide_value, slide_out, offsets,
):
    tiles = lax.axis_size("tile")
    segs = lax.axis_size("seg")
    devices = tiles * segs
    span = cached.shape[0]
    total = span * tiles
    cut, local_cols = vit_query.shape
    fresh = slide_pos.shape[0]
    padded = max(16, fresh)
    call = pl.pallas_call
    sds = jax.ShapeDtypeStruct

    here = jnp.stack([lax.axis_index("tile"), lax.axis_index("seg")]).astype(I32)
    kept_col = kept.reshape(span, 1)
    gain_vit = vit_norm_gain.reshape(1, DV)
    gain_slide = slide_gain.reshape(1, DS)

    base_rows, q_base, kv_base = call(
        base_kernel,
        out_shape=(sds((span, DS), BF16), sds((span, 256), BF16), sds((span, 384), BF16)),
        in_specs=[VMEM] * 7,
        out_specs=(VMEM,) * 3,
        compiler_params=params(),
        name="base_rows",
    )(cached, kept_col, mask_token.reshape(1, DS), gain_slide, slide_query, slide_key, slide_value)

    width = round_up(cut + fresh, 128)
    posrow = jnp.full((1, width), -1, I32).at[0, cut : cut + fresh].set(slide_pos)
    pack = call(
        functools.partial(class_kernel, fresh),
        out_shape=sds((tiles, width), F32),
        grid=(1,),
        in_specs=[
            pl.BlockSpec((1, 16, DV), lambda i: (0, 0, 0)), VMEM, VMEM, VMEM, SMEM,
        ],
        out_specs=VMEM,
        compiler_params=params(),
        name="class_row",
    )(patches, gain_vit, posrow, kept_col, here)
    pack = lax.all_to_all(pack, "tile", 0, 0, tiled=True)
    kv_all = gather_tile(kv_base)
    wv_all = gather_tile(vit_value)
    embed_all = lax.all_gather(embed_proj, "seg", axis=0)
    slide_out_all = lax.all_gather(slide_out, "seg", axis=0)

    flags = jnp.sum(pack[:, cut : cut + fresh], axis=0)
    flag_row = jnp.pad(flags, (0, padded - fresh)).reshape(1, padded)
    flag_col = flag_row.reshape(padded, 1)
    pos_pad = jnp.pad(slide_pos, (0, padded - fresh), constant_values=-1)
    pos_row, pos_col = pos_pad.reshape(1, padded), pos_pad.reshape(padded, 1)

    small = tiles <= 8
    part_shape = (tiles, fresh, local_cols) if small else (fresh, local_cols)
    part = call(
        functools.partial(query_kernel, cut),
        out_shape=sds(part_shape, F32),
        in_specs=[VMEM] * 2,
        out_specs=VMEM,
        compiler_params=params(),
        name="query_share",
    )(pack, vit_query)
    if small:
        part = lax.all_to_all(part, "tile", 0, 0, tiled=True)
    else:
        part = lax.psum(part, "tile")
    folded = call(
        fold_kernel,
        out_shape=sds((fresh, 8, round_up(cut, 128)), F32),
        in_specs=[VMEM] * 2,
        out_specs=VMEM,
        compiler_params=params(),
        name="fold_key",
    )(part, vit_key)
    folded = lax.all_to_all(folded, "tile", 0, 0, tiled=True)

    bias_row = jnp.pad(embed_bias, (0, 256 - embed_bias.shape[0])).reshape(1, 256)
    sent = call(
        functools.partial(tile_kernel, cut),
        out_shape=sds((devices, DV + 256), F32),
        in_specs=[VMEM] * 7 + [SMEM],
        out_specs=VMEM,
        scratch_shapes=[pltpu.VMEM((8, DV), F32)],
        compiler_params=params(),
        name="tile_attention",
    )(
        patches, gain_vit, folded, wv_all, vit_out, layer_scale.reshape(1, DV), bias_row, here,
    )
    shares = lax.all_to_all(sent, ("tile", "seg"), 0, 0, tiled=True)

    block = min(total, 2048)
    steps = total // block
    kv_spec = pl.BlockSpec((block, 384), lambda i: (i, 0))
    ml, acc = call(
        functools.partial(base_attention_kernel, span, total),
        out_shape=(sds((span, 128), F32), sds((span, 256), F32)),
        grid=(steps,),
        in_specs=[VMEM, kv_spec, VMEM, VMEM, SMEM, SMEM],
        out_specs=(VMEM, VMEM),
        compiler_params=params(),
        name="base_attention",
    )(q_base, kv_all, pos_col, flag_col, offsets, here)

    count = span // segs
    outs = call(
        functools.partial(fresh_kernel, span, total),
        out_shape=(sds((count, 256), BF16),) * 4 + (sds((count, DS), F32),),
        grid=(steps,),
        in_specs=[VMEM] * 8 + [kv_spec] + [VMEM] * 7 + [SMEM] * 2,
        out_specs=(VMEM,) * 5,
        scratch_shapes=[
            pltpu.VMEM((padded, DS), F32),
            pltpu.VMEM((padded, 256), BF16),
            pltpu.VMEM((padded, 384), BF16),
            pltpu.VMEM((padded, 128), F32),
            pltpu.VMEM((padded, 256), F32),
            pltpu.VMEM((span, 256), F32),
        ],
        compiler_params=params(),
        name="fresh_attention",
    )(
        shares, final_gain.reshape(1, DV), embed_all, gain_slide, slide_query, slide_key,
        slide_value, q_base, kv_all, pos_col, pos_row, flag_col, flag_row, ml, acc, base_rows,
        offsets, here,
    )
    swapped = [outs[0]] + [trade(outs[mask], "seg", mask) for mask in range(1, 4)]
    return call(
        out_kernel,
        out_shape=sds((count, DS), BF16),
        in_specs=[VMEM] * 6 + [SMEM],
        out_specs=VMEM,
        compiler_params=params(),
        name="slide_next",
    )(*swapped, slide_out_all, outs[4], here)


def solution(mesh):
    return jax.shard_map(
        shards,
        mesh=mesh,
        in_specs=(
            P("tile", None, None), P(), P("tile", "seg"), P("tile", "seg"), P("tile", "seg"),
            P("seg", None), P(), P(), P(None, "seg"), P("seg"), P(), P("tile", None), P("tile"),
            P(), P(), P(None, "seg"), P(None, "seg"), P(None, "seg"), P("seg", None), P(),
        ),
        out_specs=P(("tile", "seg"), None),
        check_vma=False,
    )
```

```python
import functools
import math

import jax
import jax.numpy as jnp
from jax import lax
from jax.experimental import pallas as pl
from jax.experimental.pallas import tpu as pltpu
from jax.sharding import PartitionSpec as P

DV = 1536
HV = 24
DS = 768
HS = 12
HEAD = 64

EPS = 1e-06
LOW = -1e30
F32 = jnp.float32
BF16 = jnp.bfloat16
I32 = jnp.int32
VMEM = pl.BlockSpec(memory_space=pltpu.VMEM)
SMEM = pl.BlockSpec(memory_space=pltpu.SMEM)
NT = (((1,), (1,)), ((), ()))
ROOM = 56 * 1024 * 1024


def params():
    return pltpu.CompilerParams(vmem_limit_bytes=ROOM)


def round_up(value, unit):
    return -(-value // unit) * unit


def layer_norm(values, scaling):
    center = values - jnp.mean(values, axis=-1, keepdims=True)
    spread = jnp.mean(center * center, axis=-1, keepdims=True)
    return center * lax.rsqrt(spread + EPS) * scaling


def dot(a, b):
    return jnp.dot(a, b, preferred_element_type=F32)


def dot_nt(a, b):
    return lax.dot_general(a, b, NT, preferred_element_type=F32)


def class_kernel(fresh, patch_ref, gain_ref, pos_ref, kept_ref, pack_ref):
    parts, _, width = pack_ref.shape
    cut = DV // parts
    rows = kept_ref.shape[0]
    row = patch_ref[0, 0:1].astype(F32)
    normed = layer_norm(row, gain_ref[...].reshape(1, DV)).astype(BF16).astype(F32)
    place = lax.broadcasted_iota(I32, (1, rows), 1) + lax.axis_index("tile") * rows
    kept = kept_ref[...].reshape(1, rows) != 0
    lane = lax.broadcasted_iota(I32, (1, width), 1)
    flags = jnp.zeros((1, width), F32)
    for index in range(fresh):
        hit = jnp.where((place == pos_ref[index]) & kept, 1.0, 0.0)
        flags = jnp.where(lane == index, jnp.max(hit, axis=1, keepdims=True), flags)
    for part in range(parts):
        pack_ref[part] = jnp.broadcast_to(flags, pack_ref.shape[1:])
        pack_ref[part, 0:1, 0:cut] = normed[:, part * cut : (part + 1) * cut]


def column(row, rows):
    width = row.shape[1]
    same = lax.broadcasted_iota(I32, (rows, width), 0) == lax.broadcasted_iota(
        I32, (rows, width), 1
    )
    return jnp.sum(jnp.where(same, row, 0.0), axis=1, keepdims=True)


def base_kernel(
    cached_ref, kept_ref, mask_ref, gain_ref, wq_ref, wk_ref, wv_ref, rows_ref, q_ref, kv_ref
):
    span = kept_ref.shape[0]
    kept = column(jnp.where(kept_ref[...].reshape(1, span) != 0, 1.0, 0.0), span)
    mask_row = mask_ref[...].reshape(1, DS).astype(BF16).astype(F32)
    rows = jnp.where(kept < 0.5, mask_row, cached_ref[...].astype(F32))
    rows_ref[...] = rows.astype(BF16)
    normed = layer_norm(rows, gain_ref[...].reshape(1, DS)).astype(BF16)
    project(normed, wq_ref, wk_ref, wv_ref, q_ref, kv_ref)


def project(normed, wq_ref, wk_ref, wv_ref, q_ref, kv_ref):
    q = dot_nt(normed, wq_ref[...]).astype(BF16) * BF16(1.0 / math.sqrt(HEAD))
    k = dot_nt(normed, wk_ref[...]).astype(BF16)
    v = dot_nt(normed, wv_ref[...]).astype(BF16)
    q_ref[:, 0:192] = q
    q_ref[:, 192:256] = jnp.zeros((q.shape[0], 64), BF16)
    kv_ref[:, 0:192] = k
    kv_ref[:, 192:256] = v[:, 128:192]
    kv_ref[:, 256:384] = v[:, 0:128]


def query_kernel(cut, pack_ref, wq_ref, part_ref):
    rows = pack_ref[:, 0, 0:cut].astype(BF16)
    part = dot(rows, wq_ref[...])
    if len(part_ref.shape) == 3:
        part_ref[...] = jnp.broadcast_to(part[None], part_ref.shape)
    else:
        part_ref[...] = part


def fold_kernel(part_ref, wk_ref, fold_ref):
    if len(part_ref.shape) == 3:
        queries = part_ref[0]
        for index in range(1, part_ref.shape[0]):
            queries = queries + part_ref[index]
    else:
        queries = part_ref[...]
    tiles, width = queries.shape
    queries = queries.astype(BF16).astype(F32)
    spread = jnp.broadcast_to(queries[:, None], (tiles, 8, width))
    head = lax.broadcasted_iota(I32, spread.shape, 1)
    lane = lax.broadcasted_iota(I32, spread.shape, 2)
    spread = jnp.where(lane // HEAD == head, spread, 0.0).reshape(tiles * 8, width).astype(BF16)
    cut = wk_ref.shape[0]
    result = dot_nt(spread, wk_ref[...]).reshape(tiles, 8, cut)
    fold_ref[:, :, 0:cut] = result
    if cut < fold_ref.shape[2]:
        fold_ref[:, :, cut:] = jnp.zeros((tiles, 8, fold_ref.shape[2] - cut), F32)


def tile_kernel(cut, patch_ref, gain_ref, fold_ref, scale_ref, bias_ref, wo_ref, *refs):
    *wv_refs, sent_ref, fold_s, mixed_s = refs
    parts = fold_ref.shape[0]
    for part in range(parts):
        fold_s[:, part * cut : (part + 1) * cut] = fold_ref[part, :, 0:cut]
    tokens = patch_ref[0].astype(F32)
    normed = layer_norm(tokens, gain_ref[...].reshape(1, DV)).astype(BF16)
    scores = dot_nt(fold_s[...].astype(BF16), normed) * (1.0 / math.sqrt(HEAD))
    highest = jnp.max(scores, axis=-1, keepdims=True)
    exponent = jnp.exp(scores - highest)
    prob = (exponent / jnp.sum(exponent, axis=-1, keepdims=True)).astype(BF16)
    mixed = dot(prob, normed)
    if len(wv_refs) == 1:
        values = dot(mixed.astype(BF16), wv_refs[0][...])
    else:
        for part in range(parts):
            mixed_s[part, :, 0:cut] = mixed[:, part * cut : (part + 1) * cut]
        values = jnp.zeros((8, wo_ref.shape[0]), F32)
        me = lax.axis_index("tile")
        for low, ref in enumerate(wv_refs):
            for high in range(parts // 2):
                piece = mixed_s[me ^ (2 * high + low)][:, 0:cut].astype(BF16)
                values = values + dot(piece, ref[high * cut : (high + 1) * cut])
    head = lax.broadcasted_iota(I32, values.shape, 0)
    lane = lax.broadcasted_iota(I32, values.shape, 1)
    tmix = jnp.sum(jnp.where(lane // HEAD == head, values, 0.0), axis=0, keepdims=True)
    tmix = jnp.broadcast_to(tmix, (8, tmix.shape[1])).astype(BF16)
    share = dot(tmix, wo_ref[...])[0:1] * scale_ref[...].reshape(1, DV)
    share = share + jnp.where(lax.axis_index("seg") == 0, tokens[0:1], 0.0)
    devices = sent_ref.shape[0]
    for row in range(DV // 256):
        piece = share[:, None, row * 256 : (row + 1) * 256]
        sent_ref[:, row : row + 1, :] = jnp.broadcast_to(piece, (devices, 1, 256))
    width = bias_ref.shape[0]
    bias = bias_ref[...].reshape(1, 1, width)
    sent_ref[:, 6:8, :] = jnp.zeros((devices, 2, 256), F32)
    sent_ref[:, 6:7, 0:width] = jnp.broadcast_to(bias, (devices, 1, width))


def branch_rows(position, axis, offset_ref, head, span, total):
    shape = (1, 8) if axis == 1 else (8, 1)
    branch = lax.broadcasted_iota(I32, shape, axis)
    residue = jnp.full(shape, -1, I32)
    shift = jnp.zeros(shape, I32)
    for b in range(offset_ref.shape[0]):
        residue = jnp.where(branch == b, offset_ref[b, lax.axis_index("seg") * 3 + head], residue)
        length = min(2 * span * 4**b, total)
        shift = jnp.where(branch == b, length.bit_length() - 1, shift)
    below = jnp.left_shift(jnp.int32(1), branch) - 1
    mine = jnp.right_shift(jnp.zeros(shape, I32) + lax.axis_index("tile") * span, shift)
    return ((position & below) == residue) & (jnp.right_shift(position, shift) == mine)


def value_lanes(head):
    group = {0: 2, 1: 3, 2: 1}[head]
    lane = lax.broadcasted_iota(I32, (1, 256), 1)
    return lane // HEAD == group


def attend(q, q_rows, kv_ref, k_rows, head):
    lane = lax.broadcasted_iota(I32, (1, 256), 1)
    q_head = jnp.where(lane // HEAD == head, q, jnp.zeros_like(q))
    scores = dot_nt(q_head, kv_ref[:, 0:256])
    count = dot(q_rows, k_rows)
    scores = jnp.where(count > 0.5, scores, LOW)
    highest = jnp.max(scores, axis=-1, keepdims=True)
    weight = jnp.exp(scores - highest) * count
    denom = jnp.sum(weight, axis=-1, keepdims=True)
    numer = dot(weight.astype(BF16), kv_ref[:, 128:384])
    return highest, denom, numer


def as_bf16(condition):
    return jnp.where(condition, 1.0, 0.0).astype(BF16)


def merge(old, new):
    old_max, old_den, old_num = old
    new_max, new_den, new_num = new
    top = jnp.maximum(old_max, new_max)
    keep = jnp.exp(old_max - top)
    take = jnp.exp(new_max - top)
    return top, old_den * keep + new_den * take, old_num * keep + new_num * take


def store_state(state, head, ml_ref, acc_ref):
    highest, denom, numer = state
    lane = lax.broadcasted_iota(I32, (1, 128), 1)
    ml = jnp.where(lane == head, highest, ml_ref[...])
    ml_ref[...] = jnp.where(lane == head + 8, denom, ml)
    acc_ref[...] = jnp.where(value_lanes(head), numer, acc_ref[...])


def load_state(head, ml_ref, acc_ref):
    return ml_ref[:, head : head + 1], ml_ref[:, head + 8 : head + 9], acc_ref[...]


def fresh_places(padded, pack_ref, pos_ref):
    flags = pack_ref[0, 1:2, :]
    for part in range(1, pack_ref.shape[0]):
        flags = flags + pack_ref[part, 1:2, :]
    flag_col = column(flags, padded)
    lane = lax.broadcasted_iota(I32, (1, padded), 1)
    sub = lax.broadcasted_iota(I32, (padded, 1), 0)
    row = jnp.full((1, padded), -1, I32)
    col = jnp.full((padded, 1), -1, I32)
    for index in range(pos_ref.shape[0]):
        row = jnp.where(lane == index, pos_ref[index], row)
        col = jnp.where(sub == index, pos_ref[index], col)
    return row, col, flags[:, 0:padded] > 0.5, flag_col > 0.5


def key_places(swapped, low, block, span, step):
    place = lax.broadcasted_iota(I32, (1, block), 1)
    if not swapped:
        return place + step * block
    source = lax.axis_index("tile") ^ (2 * (place // span) + low)
    return source * span + (place & (span - 1))


def key_rows(place, pos_col, flag_col, offset_ref, head, span, total):
    rows = branch_rows(place, 0, offset_ref, head, span, total)
    taken = jnp.where((place == pos_col) & flag_col, 1.0, 0.0)
    taken = jnp.max(taken, axis=0, keepdims=True)
    return as_bf16(rows & (taken < 0.5))


def base_attention_kernel(span, total, padded, pos_ref, offset_ref, pack_ref, q_ref, *refs):
    *kv_refs, ml_ref, acc_ref = refs
    step = pl.program_id(0)
    rows = q_ref.shape[0]

    @pl.when(step == 0)
    def _():
        lane = lax.broadcasted_iota(I32, (rows, 128), 1)
        ml_ref[...] = jnp.where(lane < 8, LOW, 0.0)
        acc_ref[...] = jnp.zeros_like(acc_ref)

    _, pos_col, _, flag_col = fresh_places(padded, pack_ref, pos_ref)
    place = lax.broadcasted_iota(I32, (rows, 1), 0) + lax.axis_index("tile") * span
    for head in range(3):
        q_rows = as_bf16(branch_rows(place, 1, offset_ref, head, span, total))
        for low, kv_ref in enumerate(kv_refs):
            keys = key_places(len(kv_refs) > 1, low, kv_ref.shape[0], span, step)
            k_rows = key_rows(keys, pos_col, flag_col, offset_ref, head, span, total)
            new = attend(q_ref[...], q_rows, kv_ref, k_rows, head)
            store_state(merge(load_state(head, ml_ref, acc_ref), new), head, ml_ref, acc_ref)


def fresh_kernel(
    span, total, parts, pos_ref, offset_ref, pack_ref, q_ref, shares_ref, final_ref, gain_ref,
    wq_ref, wk_ref, wv_ref, ml_ref, acc_ref, rows_ref, *refs,
):
    embed_refs, refs = refs[:4], refs[4:]
    kv_refs, refs = refs[:parts], refs[parts:]
    outs, refs = refs[:4], refs[4:]
    mine_ref, fresh_s, qf_s, kvf_s, mlf_s, accf_s, att_s = refs
    step = pl.program_id(0)
    rows = q_ref.shape[0]
    padded = fresh_s.shape[0]
    seg = lax.axis_index("seg")
    pos_row, pos_col, flag_row, flag_col = fresh_places(padded, pack_ref, pos_ref)

    @pl.when(step == 0)
    def _():
        groups = shares_ref.shape[0] // 4
        pooled = []
        for row in range(DV // 256):
            pooled.append(jnp.sum(shares_ref[:, row, :].reshape(groups, 4, 256), axis=1))
        pooled = jnp.concatenate(pooled, axis=1)
        summary = layer_norm(pooled, final_ref[...].reshape(1, DV)).astype(BF16)
        fresh_s[...] = jnp.zeros_like(fresh_s)
        pieces = [dot_nt(summary, ref[...]) for ref in embed_refs]
        for part in range(4):
            piece = pieces[0]
            for mask in range(1, 4):
                piece = jnp.where((seg ^ part) == mask, pieces[mask], piece)
            piece = piece + shares_ref[part, 6:7, 0:192]
            fresh_s[0:groups, part * 192 : (part + 1) * 192] = piece.astype(BF16).astype(F32)
        normed = layer_norm(fresh_s[...], gain_ref[...].reshape(1, DS)).astype(BF16)
        project(normed, wq_ref, wk_ref, wv_ref, qf_s, kvf_s)
        lane = lax.broadcasted_iota(I32, (padded, 128), 1)
        mlf_s[...] = jnp.where(lane < 8, LOW, 0.0)
        accf_s[...] = jnp.zeros_like(accf_s)

    for head in range(3):
        q_rows = as_bf16(branch_rows(pos_col, 1, offset_ref, head, span, total))
        for low, kv_ref in enumerate(kv_refs):
            keys = key_places(parts > 1, low, kv_ref.shape[0], span, step)
            k_rows = key_rows(keys, pos_col, flag_col, offset_ref, head, span, total)
            new = attend(qf_s[...], q_rows, kv_ref, k_rows, head)
            store_state(merge(load_state(head, mlf_s, accf_s), new), head, mlf_s, accf_s)

    @pl.when(step == pl.num_programs(0) - 1)
    def _():
        first = lax.axis_index("tile") * span
        place = lax.broadcasted_iota(I32, (rows, 1), 0) + first
        base = jnp.zeros((rows, 256), F32)
        fresh = jnp.zeros((padded, 256), F32)
        for head in range(3):
            q_rows = as_bf16(branch_rows(place, 1, offset_ref, head, span, total))
            f_rows = as_bf16(branch_rows(pos_col, 1, offset_ref, head, span, total))
            k_rows = as_bf16(branch_rows(pos_row, 0, offset_ref, head, span, total) & flag_row)
            lanes = value_lanes(head)
            new = attend(q_ref[...], q_rows, kvf_s, k_rows, head)
            top, den, num = merge(load_state(head, ml_ref, acc_ref), new)
            base = jnp.where(lanes, num / den, base)
            new = attend(qf_s[...], f_rows, kvf_s, k_rows, head)
            top, den, num = merge(load_state(head, mlf_s, accf_s), new)
            fresh = jnp.where(lanes, num / jnp.where(den > 0.0, den, 1.0), fresh)
        chosen = as_bf16((place == pos_row) & flag_row)
        hit = jnp.sum(chosen.astype(F32), axis=1, keepdims=True) > 0.5
        att_s[...] = jnp.where(hit, dot(chosen, fresh.astype(BF16)), base)
        count = rows // 4
        for mask in range(4):
            start = pl.multiple_of((seg ^ mask) * count, count)
            outs[mask][...] = att_s[pl.ds(start, count), :].astype(BF16)
        start = pl.multiple_of(seg * count, count)
        place = lax.broadcasted_iota(I32, (count, 1), 0) + first + start
        chosen = as_bf16((place == pos_row) & flag_row)
        hit = jnp.sum(chosen.astype(F32), axis=1, keepdims=True) > 0.5
        placed = dot(chosen, fresh_s[...].astype(BF16))
        old = rows_ref[pl.ds(start, count), :].astype(F32)
        mine_ref[...] = jnp.where(hit, placed, old)


def out_kernel(mine_ref, *refs):
    out_ref = refs[8]
    total = mine_ref[...]
    for mask in range(4):
        att, weight = refs[mask][...], refs[4 + mask]
        total = total + dot(att[:, 128:256], weight[0:128])
        total = total + dot(att[:, 64:128], weight[128:192])
    out_ref[...] = total.astype(BF16)


def trade(block, axis, mask):
    count = lax.axis_size(axis)
    return lax.ppermute(block, axis, [(i, i ^ mask) for i in range(count)])


def gather_tile(block):
    count = lax.axis_size("tile")
    if count > 8:
        return [lax.all_gather(block, "tile", axis=0, tiled=True)]
    parts = [block] + [trade(block, "tile", mask) for mask in range(2, count, 2)]
    even = jnp.concatenate(parts, axis=0)
    return [even, trade(even, "tile", 1)]


def gather_seg(block):
    return [block] + [trade(block, "seg", mask) for mask in range(1, 4)]


def shards(
    patches, vit_norm_gain, vit_query, vit_key, vit_value, vit_out, layer_scale, final_gain,
    embed_proj, embed_bias, slide_pos, cached, kept, mask_token, slide_gain, slide_query,
    slide_key, slide_value, slide_out, offsets,
):
    tiles = lax.axis_size("tile")
    segs = lax.axis_size("seg")
    devices = tiles * segs
    span = cached.shape[0]
    total = span * tiles
    cut, local_cols = vit_query.shape
    fresh = slide_pos.shape[0]
    padded = max(16, fresh)
    call = pl.pallas_call
    sds = jax.ShapeDtypeStruct
    weights = (slide_query.T, slide_key.T, slide_value.T)

    pack = call(
        functools.partial(class_kernel, fresh),
        out_shape=sds((tiles, 8, 256), F32),
        grid=(1,),
        in_specs=[pl.BlockSpec((1, 16, DV), lambda i: (0, 0, 0)), VMEM, SMEM, VMEM],
        out_specs=VMEM,
        compiler_params=params(),
        name="class_row",
    )(patches, vit_norm_gain, slide_pos, kept)
    pack = lax.all_to_all(pack, "tile", 0, 0, tiled=True)

    base_rows, q_base, kv_base = call(
        base_kernel,
        out_shape=(sds((span, DS), BF16), sds((span, 256), BF16), sds((span, 384), BF16)),
        in_specs=[VMEM] * 7,
        out_specs=(VMEM,) * 3,
        compiler_params=params(),
        name="base_rows",
    )(cached, kept, mask_token, slide_gain, *weights)
    wv_all = gather_tile(vit_value)
    kv_all = gather_tile(kv_base)
    embed_all = gather_seg(embed_proj.T)
    slide_out_all = gather_seg(slide_out)

    small = tiles <= 8
    part_shape = (tiles, fresh, local_cols) if small else (fresh, local_cols)
    part = call(
        functools.partial(query_kernel, cut),
        out_shape=sds(part_shape, F32),
        in_specs=[VMEM] * 2,
        out_specs=VMEM,
        compiler_params=params(),
        name="query_share",
    )(pack, vit_query)
    if small:
        part = lax.all_to_all(part, "tile", 0, 0, tiled=True)
    else:
        part = lax.psum(part, "tile")
    folded = call(
        fold_kernel,
        out_shape=sds((fresh, 8, round_up(cut, 128)), F32),
        in_specs=[VMEM] * 2,
        out_specs=VMEM,
        compiler_params=params(),
        name="fold_key",
    )(part, vit_key)
    folded = lax.all_to_all(folded, "tile", 0, 0, tiled=True)

    sent = call(
        functools.partial(tile_kernel, cut),
        out_shape=sds((devices, 8, 256), F32),
        in_specs=[VMEM] * (6 + len(wv_all)),
        out_specs=VMEM,
        scratch_shapes=[
            pltpu.VMEM((8, DV), F32), pltpu.VMEM((tiles, 8, round_up(cut, 128)), F32),
        ],
        compiler_params=params(),
        name="tile_attention",
    )(patches, vit_norm_gain, folded, layer_scale, embed_bias, vit_out, *wv_all)
    shares = lax.all_to_all(sent, ("tile", "seg"), 0, 0, tiled=True)

    parts = len(kv_all)
    block = min(kv_all[0].shape[0], 2048)
    steps = kv_all[0].shape[0] // block
    kv_specs = [pl.BlockSpec((block, 384), lambda i: (i, 0))] * parts
    ml, acc = call(
        functools.partial(base_attention_kernel, span, total, padded),
        out_shape=(sds((span, 128), F32), sds((span, 256), F32)),
        grid=(steps,),
        in_specs=[SMEM, SMEM, VMEM, VMEM] + kv_specs,
        out_specs=(VMEM, VMEM),
        compiler_params=params(),
        name="base_attention",
    )(slide_pos, offsets, pack, q_base, *kv_all)

    count = span // segs
    outs = call(
        functools.partial(fresh_kernel, span, total, parts),
        out_shape=(sds((count, 256), BF16),) * 4 + (sds((count, DS), F32),),
        grid=(steps,),
        in_specs=[SMEM] * 2 + [VMEM] * 15 + kv_specs,
        out_specs=(VMEM,) * 5,
        scratch_shapes=[
            pltpu.VMEM((padded, DS), F32),
            pltpu.VMEM((padded, 256), BF16),
            pltpu.VMEM((padded, 384), BF16),
            pltpu.VMEM((padded, 128), F32),
            pltpu.VMEM((padded, 256), F32),
            pltpu.VMEM((span, 256), F32),
        ],
        compiler_params=params(),
        name="fresh_attention",
    )(
        slide_pos, offsets, pack, q_base, shares, final_gain, slide_gain, *weights, ml, acc,
        base_rows, *embed_all, *kv_all,
    )
    swapped = [outs[0]] + [trade(outs[mask], "seg", mask) for mask in range(1, 4)]
    return call(
        out_kernel,
        out_shape=sds((count, DS), BF16),
        in_specs=[VMEM] * 9,
        out_specs=VMEM,
        compiler_params=params(),
        name="slide_next",
    )(outs[4], *swapped, *slide_out_all)


def solution(mesh):
    return jax.shard_map(
        shards,
        mesh=mesh,
        in_specs=(
            P("tile", None, None), P(), P("tile", "seg"), P("tile", "seg"), P("tile", "seg"),
            P("seg", None), P(), P(), P(None, "seg"), P("seg"), P(), P("tile", None), P("tile"),
            P(), P(), P(None, "seg"), P(None, "seg"), P(None, "seg"), P("seg", None), P(),
        ),
        out_specs=P(("tile", "seg"), None),
        check_vma=False,
    )
```

```python
import functools
import math

import jax
import jax.numpy as jnp
from jax import lax
from jax.experimental import pallas as pl
from jax.experimental.pallas import tpu as pltpu
from jax.sharding import PartitionSpec as P

DV = 1536
HV = 24
DS = 768
HS = 12
HEAD = 64

EPS = 1e-06
LOW = -1e30
F32 = jnp.float32
BF16 = jnp.bfloat16
I32 = jnp.int32
VMEM = pl.BlockSpec(memory_space=pltpu.VMEM)
SMEM = pl.BlockSpec(memory_space=pltpu.SMEM)
NT = (((1,), (1,)), ((), ()))
MIB = 1024 * 1024


def params(room):
    return pltpu.CompilerParams(vmem_limit_bytes=room * MIB)


def round_up(value, unit):
    return -(-value // unit) * unit


def layer_norm(values, scaling):
    center = values - jnp.mean(values, axis=-1, keepdims=True)
    spread = jnp.mean(center * center, axis=-1, keepdims=True)
    return center * lax.rsqrt(spread + EPS) * scaling


def dot(a, b):
    return jnp.dot(a, b, preferred_element_type=F32)


def dot_nt(a, b):
    return lax.dot_general(a, b, NT, preferred_element_type=F32)


def class_kernel(fresh, patch_ref, gain_ref, pos_ref, kept_ref, pack_ref):
    parts, _, width = pack_ref.shape
    cut = DV // parts
    rows = kept_ref.shape[0]
    row = patch_ref[0, 0:1].astype(F32)
    normed = layer_norm(row, gain_ref[...].reshape(1, DV)).astype(BF16).astype(F32)
    place = lax.broadcasted_iota(I32, (1, rows), 1) + lax.axis_index("tile") * rows
    kept = kept_ref[...].reshape(1, rows) != 0
    lane = lax.broadcasted_iota(I32, (1, width), 1)
    flags = jnp.zeros((1, width), F32)
    for index in range(fresh):
        hit = jnp.where((place == pos_ref[index]) & kept, 1.0, 0.0)
        flags = jnp.where(lane == index, jnp.max(hit, axis=1, keepdims=True), flags)
    for part in range(parts):
        pack_ref[part] = jnp.broadcast_to(flags, pack_ref.shape[1:])
        pack_ref[part, 0:1, 0:cut] = normed[:, part * cut : (part + 1) * cut]


def column(row, rows):
    width = row.shape[1]
    same = lax.broadcasted_iota(I32, (rows, width), 0) == lax.broadcasted_iota(
        I32, (rows, width), 1
    )
    return jnp.sum(jnp.where(same, row, 0.0), axis=1, keepdims=True)


def base_kernel(
    cached_ref, kept_ref, mask_ref, gain_ref, wq_ref, wk_ref, wv_ref, rows_ref, q_ref, kv_ref
):
    span = kept_ref.shape[0]
    kept = column(jnp.where(kept_ref[...].reshape(1, span) != 0, 1.0, 0.0), span)
    mask_row = mask_ref[...].reshape(1, DS).astype(BF16).astype(F32)
    rows = jnp.where(kept < 0.5, mask_row, cached_ref[...].astype(F32))
    rows_ref[...] = rows.astype(BF16)
    normed = layer_norm(rows, gain_ref[...].reshape(1, DS)).astype(BF16)
    project(normed, wq_ref, wk_ref, wv_ref, q_ref, kv_ref)


def project(normed, wq_ref, wk_ref, wv_ref, q_ref, kv_ref):
    q = dot_nt(normed, wq_ref[...]).astype(BF16) * BF16(1.0 / math.sqrt(HEAD))
    k = dot_nt(normed, wk_ref[...]).astype(BF16)
    v = dot_nt(normed, wv_ref[...]).astype(BF16)
    q_ref[:, 0:192] = q
    q_ref[:, 192:256] = jnp.zeros((q.shape[0], 64), BF16)
    kv_ref[:, 0:192] = k
    kv_ref[:, 192:256] = v[:, 128:192]
    kv_ref[:, 256:384] = v[:, 0:128]


def query_kernel(cut, pack_ref, wq_ref, part_ref):
    rows = pack_ref[:, 0, 0:cut].astype(BF16)
    part = dot(rows, wq_ref[...])
    if len(part_ref.shape) == 3:
        part_ref[...] = jnp.broadcast_to(part[None], part_ref.shape)
    else:
        part_ref[...] = part


def fold_kernel(part_ref, wk_ref, fold_ref):
    if len(part_ref.shape) == 3:
        queries = part_ref[0]
        for index in range(1, part_ref.shape[0]):
            queries = queries + part_ref[index]
    else:
        queries = part_ref[...]
    tiles, width = queries.shape
    queries = queries.astype(BF16).astype(F32)
    spread = jnp.broadcast_to(queries[:, None], (tiles, 8, width))
    head = lax.broadcasted_iota(I32, spread.shape, 1)
    lane = lax.broadcasted_iota(I32, spread.shape, 2)
    spread = jnp.where(lane // HEAD == head, spread, 0.0).reshape(tiles * 8, width).astype(BF16)
    cut = wk_ref.shape[0]
    result = dot_nt(spread, wk_ref[...]).reshape(tiles, 8, cut)
    fold_ref[:, :, 0:cut] = result
    if cut < fold_ref.shape[2]:
        fold_ref[:, :, cut:] = jnp.zeros((tiles, 8, fold_ref.shape[2] - cut), F32)


def tile_kernel(cut, patch_ref, gain_ref, fold_ref, scale_ref, bias_ref, wo_ref, *refs):
    *wv_refs, sent_ref, fold_s, mixed_s = refs
    parts = fold_ref.shape[0]
    for part in range(parts):
        fold_s[:, part * cut : (part + 1) * cut] = fold_ref[part, :, 0:cut]
    tokens = patch_ref[0].astype(F32)
    normed = layer_norm(tokens, gain_ref[...].reshape(1, DV)).astype(BF16)
    scores = dot_nt(fold_s[...].astype(BF16), normed) * (1.0 / math.sqrt(HEAD))
    highest = jnp.max(scores, axis=-1, keepdims=True)
    exponent = jnp.exp(scores - highest)
    prob = (exponent / jnp.sum(exponent, axis=-1, keepdims=True)).astype(BF16)
    mixed = dot(prob, normed)
    if len(wv_refs) == 1:
        values = dot(mixed.astype(BF16), wv_refs[0][...])
    else:
        for part in range(parts):
            mixed_s[part, :, 0:cut] = mixed[:, part * cut : (part + 1) * cut]
        values = jnp.zeros((8, wo_ref.shape[0]), F32)
        me = lax.axis_index("tile")
        for masks, ref in zip(GROUPS, wv_refs):
            for index, mask in enumerate(masks):
                piece = mixed_s[me ^ mask][:, 0:cut].astype(BF16)
                values = values + dot(piece, ref[index * cut : (index + 1) * cut])
    head = lax.broadcasted_iota(I32, values.shape, 0)
    lane = lax.broadcasted_iota(I32, values.shape, 1)
    tmix = jnp.sum(jnp.where(lane // HEAD == head, values, 0.0), axis=0, keepdims=True)
    tmix = jnp.broadcast_to(tmix, (8, tmix.shape[1])).astype(BF16)
    share = dot(tmix, wo_ref[...])[0:1] * scale_ref[...].reshape(1, DV)
    share = share + jnp.where(lax.axis_index("seg") == 0, tokens[0:1], 0.0)
    devices = sent_ref.shape[0]
    for row in range(DV // 256):
        piece = share[:, None, row * 256 : (row + 1) * 256]
        sent_ref[:, row : row + 1, :] = jnp.broadcast_to(piece, (devices, 1, 256))
    width = bias_ref.shape[0]
    bias = bias_ref[...].reshape(1, 1, width)
    sent_ref[:, 6:8, :] = jnp.zeros((devices, 2, 256), F32)
    sent_ref[:, 6:7, 0:width] = jnp.broadcast_to(bias, (devices, 1, width))


def branch_rows(position, axis, offset_ref, span, total):
    shape = (1, 24) if axis == 1 else (24, 1)
    index = lax.broadcasted_iota(I32, shape, axis)
    branch = index % 8
    residue = jnp.full(shape, -1, I32)
    shift = jnp.zeros(shape, I32)
    for b in range(offset_ref.shape[0]):
        for head in range(3):
            offset = offset_ref[b, lax.axis_index("seg") * 3 + head]
            residue = jnp.where(index == head * 8 + b, offset, residue)
        length = min(2 * span * 4**b, total)
        shift = jnp.where(branch == b, length.bit_length() - 1, shift)
    below = jnp.left_shift(jnp.int32(1), branch) - 1
    mine = jnp.right_shift(jnp.zeros(shape, I32) + lax.axis_index("tile") * span, shift)
    return ((position & below) == residue) & (jnp.right_shift(position, shift) == mine)


def as_bf16(condition):
    return jnp.where(condition, 1.0, 0.0).astype(BF16)


def stack_heads(values, size):
    lane = lax.broadcasted_iota(I32, (1, values.shape[1]), 1)
    zero = jnp.zeros_like(values)
    return jnp.concatenate(
        [jnp.where(lane // size == head, values, zero) for head in range(3)], axis=0
    )


def attend(q, q_rows, kv_ref, k_rows):
    scores = dot_nt(stack_heads(q, HEAD), kv_ref[:, 0:256])
    count = dot(stack_heads(as_bf16(q_rows), 8), k_rows)
    scores = jnp.where(count > 0.5, scores, LOW)
    highest = jnp.max(scores, axis=-1, keepdims=True)
    weight = jnp.exp(scores - highest) * count
    denom = jnp.sum(weight, axis=-1, keepdims=True)
    numer = dot(weight.astype(BF16), kv_ref[:, 128:384])
    return highest, denom, numer


def merge(old, new):
    old_max, old_den, old_num = old
    new_max, new_den, new_num = new
    top = jnp.maximum(old_max, new_max)
    keep = jnp.exp(old_max - top)
    take = jnp.exp(new_max - top)
    return top, old_den * keep + new_den * take, old_num * keep + new_num * take


def clear_state(ml_ref, acc_ref):
    lane = lax.broadcasted_iota(I32, ml_ref.shape, 1)
    ml_ref[...] = jnp.where(lane == 0, LOW, 0.0)
    acc_ref[...] = jnp.zeros_like(acc_ref)


def store_state(state, ml_ref, acc_ref):
    highest, denom, numer = state
    lane = lax.broadcasted_iota(I32, ml_ref.shape, 1)
    ml_ref[...] = jnp.where(lane == 0, highest, denom)
    acc_ref[...] = numer


def load_state(ml_ref, acc_ref):
    return ml_ref[:, 0:1], ml_ref[:, 1:2], acc_ref[...]


def finish(state):
    _, den, num = state
    result = num / jnp.where(den > 0.0, den, 1.0)
    rows = num.shape[0] // 3
    group = lax.broadcasted_iota(I32, (1, 256), 1) // HEAD
    joined = jnp.where(group == 1, result[2 * rows :], 0.0)
    joined = jnp.where(group == 2, result[0:rows], joined)
    return jnp.where(group == 3, result[rows : 2 * rows], joined)


def fresh_places(padded, pack_ref, pos_ref):
    flags = pack_ref[0, 1:2, :]
    for part in range(1, pack_ref.shape[0]):
        flags = flags + pack_ref[part, 1:2, :]
    flag_col = column(flags, padded)
    lane = lax.broadcasted_iota(I32, (1, padded), 1)
    sub = lax.broadcasted_iota(I32, (padded, 1), 0)
    row = jnp.full((1, padded), -1, I32)
    col = jnp.full((padded, 1), -1, I32)
    for index in range(pos_ref.shape[0]):
        row = jnp.where(lane == index, pos_ref[index], row)
        col = jnp.where(sub == index, pos_ref[index], col)
    return row, col, flags[:, 0:padded] > 0.5, flag_col > 0.5


def key_places(swapped, block, span, step):
    place = lax.broadcasted_iota(I32, (1, block), 1)
    if not swapped:
        return place + step * block
    part = place // span
    mask = jnp.where(part < 4, 2 * part, 2 * part - 7)
    return (lax.axis_index("tile") ^ mask) * span + (place & (span - 1))


def key_rows(place, pos_col, flag_col, offset_ref, span, total):
    rows = branch_rows(place, 0, offset_ref, span, total)
    taken = jnp.where((place == pos_col) & flag_col, 1.0, 0.0)
    taken = jnp.max(taken, axis=0, keepdims=True)
    return as_bf16(rows & (taken < 0.5))


def base_attention_kernel(span, total, padded, pos_ref, offset_ref, pack_ref, q_ref, *refs):
    *kv_refs, krows_ref, ml_ref, acc_ref = refs
    swapped = len(kv_refs) > 1
    kv_ref = kv_refs.pop()
    step = pl.program_id(0)
    rows = q_ref.shape[0]
    block = kv_ref.shape[0]

    @pl.when(step == 0)
    def _():
        clear_state(ml_ref, acc_ref)

    start = 0
    for ref in kv_refs:
        kv_ref[start : start + ref.shape[0], :] = ref[...]
        start += ref.shape[0]
    _, pos_col, _, flag_col = fresh_places(padded, pack_ref, pos_ref)
    place = lax.broadcasted_iota(I32, (rows, 1), 0) + lax.axis_index("tile") * span
    q_rows = branch_rows(place, 1, offset_ref, span, total)
    keys = key_places(swapped, block, span, step)
    k_rows = key_rows(keys, pos_col, flag_col, offset_ref, span, total)
    krows_ref[...] = k_rows
    new = attend(q_ref[...], q_rows, kv_ref, k_rows)
    store_state(merge(load_state(ml_ref, acc_ref), new), ml_ref, acc_ref)


def fresh_kernel(
    span, total, pos_ref, offset_ref, pack_ref, q_ref, shares_ref, final_ref, gain_ref,
    wq_ref, wk_ref, wv_ref, ml_ref, acc_ref, rows_ref, *refs,
):
    embed_refs, refs = refs[:4], refs[4:]
    kv_ref, krows_ref, *refs = refs
    outs, refs = refs[:4], refs[4:]
    mine_ref, fresh_s, qf_s, kvf_s, mlf_s, accf_s, att_s = refs
    step = pl.program_id(0)
    rows = q_ref.shape[0]
    padded = fresh_s.shape[0]
    seg = lax.axis_index("seg")
    pos_row, pos_col, flag_row, flag_col = fresh_places(padded, pack_ref, pos_ref)
    f_rows = branch_rows(pos_col, 1, offset_ref, span, total)

    @pl.when(step == 0)
    def _():
        groups = shares_ref.shape[0] // 4
        pooled = []
        for row in range(DV // 256):
            pooled.append(jnp.sum(shares_ref[:, row, :].reshape(groups, 4, 256), axis=1))
        pooled = jnp.concatenate(pooled, axis=1)
        summary = layer_norm(pooled, final_ref[...].reshape(1, DV)).astype(BF16)
        fresh_s[...] = jnp.zeros_like(fresh_s)
        pieces = [dot_nt(summary, ref[...]) for ref in embed_refs]
        for part in range(4):
            piece = pieces[0]
            for mask in range(1, 4):
                piece = jnp.where((seg ^ part) == mask, pieces[mask], piece)
            piece = piece + shares_ref[part, 6:7, 0:192]
            fresh_s[0:groups, part * 192 : (part + 1) * 192] = piece.astype(BF16).astype(F32)
        normed = layer_norm(fresh_s[...], gain_ref[...].reshape(1, DS)).astype(BF16)
        project(normed, wq_ref, wk_ref, wv_ref, qf_s, kvf_s)
        clear_state(mlf_s, accf_s)

    new = attend(qf_s[...], f_rows, kv_ref, krows_ref[...])
    store_state(merge(load_state(mlf_s, accf_s), new), mlf_s, accf_s)

    @pl.when(step == pl.num_programs(0) - 1)
    def _():
        first = lax.axis_index("tile") * span
        place = lax.broadcasted_iota(I32, (rows, 1), 0) + first
        q_rows = branch_rows(place, 1, offset_ref, span, total)
        k_rows = as_bf16(branch_rows(pos_row, 0, offset_ref, span, total) & flag_row)
        new = attend(q_ref[...], q_rows, kvf_s, k_rows)
        base = finish(merge(load_state(ml_ref, acc_ref), new))
        new = attend(qf_s[...], f_rows, kvf_s, k_rows)
        fresh = finish(merge(load_state(mlf_s, accf_s), new))
        chosen = as_bf16((place == pos_row) & flag_row)
        hit = jnp.sum(chosen.astype(F32), axis=1, keepdims=True) > 0.5
        att_s[...] = jnp.where(hit, dot(chosen, fresh.astype(BF16)), base)
        count = rows // 4
        for mask in range(4):
            start = pl.multiple_of((seg ^ mask) * count, count)
            outs[mask][...] = att_s[pl.ds(start, count), :].astype(BF16)
        start = pl.multiple_of(seg * count, count)
        place = lax.broadcasted_iota(I32, (count, 1), 0) + first + start
        chosen = as_bf16((place == pos_row) & flag_row)
        hit = jnp.sum(chosen.astype(F32), axis=1, keepdims=True) > 0.5
        placed = dot(chosen, fresh_s[...].astype(BF16))
        old = rows_ref[pl.ds(start, count), :].astype(F32)
        mine_ref[...] = jnp.where(hit, placed, old)


def out_kernel(mine_ref, *refs):
    out_ref = refs[8]
    total = mine_ref[...]
    for mask in range(4):
        att, weight = refs[mask][...], refs[4 + mask]
        total = total + dot(att[:, 128:256], weight[0:128])
        total = total + dot(att[:, 64:128], weight[128:192])
    out_ref[...] = total.astype(BF16)


def trade(block, axis, mask):
    count = lax.axis_size(axis)
    return lax.ppermute(block, axis, [(i, i ^ mask) for i in range(count)])


GROUPS = ((0,), (2, 4, 6), (1,), (3, 5, 7))


def together(*values):
    return lax.optimization_barrier(values)


def shards(
    patches, vit_norm_gain, vit_query, vit_key, vit_value, vit_out, layer_scale, final_gain,
    embed_proj, embed_bias, slide_pos, cached, kept, mask_token, slide_gain, slide_query,
    slide_key, slide_value, slide_out, offsets,
):
    tiles = lax.axis_size("tile")
    segs = lax.axis_size("seg")
    devices = tiles * segs
    span = cached.shape[0]
    total = span * tiles
    cut, local_cols = vit_query.shape
    fresh = slide_pos.shape[0]
    padded = max(16, fresh)
    small = tiles == 8
    call = pl.pallas_call
    sds = jax.ShapeDtypeStruct
    weights = (slide_query.T, slide_key.T, slide_value.T)
    embed = embed_proj.T

    pack = call(
        functools.partial(class_kernel, fresh),
        out_shape=sds((tiles, 8, 256), F32),
        grid=(1,),
        in_specs=[pl.BlockSpec((1, 16, DV), lambda i: (0, 0, 0)), VMEM, SMEM, VMEM],
        out_specs=VMEM,
        compiler_params=params(8),
        name="class_row",
    )(patches, vit_norm_gain, slide_pos, kept)

    pack, value, cached, embed, slide_out = together(pack, vit_value, cached, embed, slide_out)
    pack = lax.all_to_all(pack, "tile", 0, 0, tiled=True)
    base_rows, q_base, kv_base = call(
        base_kernel,
        out_shape=(sds((span, DS), BF16), sds((span, 256), BF16), sds((span, 384), BF16)),
        in_specs=[VMEM] * 7,
        out_specs=(VMEM,) * 3,
        compiler_params=params(16),
        name="base_rows",
    )(cached, kept, mask_token, slide_gain, *weights)
    if small:
        value_z = [trade(value, "tile", mask) for mask in (2, 4, 6)]
        value_y = trade(value, "tile", 1)
        kv_y = trade(kv_base, "tile", 1)
    embed_x = trade(embed, "seg", 2)
    out_x = trade(slide_out, "seg", 2)

    part_shape = (tiles, fresh, local_cols) if small else (fresh, local_cols)
    part = call(
        functools.partial(query_kernel, cut),
        out_shape=sds(part_shape, F32),
        in_specs=[VMEM] * 2,
        out_specs=VMEM,
        compiler_params=params(8 if small else 16),
        name="query_share",
    )(pack, vit_query)
    if small:
        value_z = jnp.concatenate(value_z, axis=0)
        part, value_z, kv_own, embed, embed_x, slide_out, out_x = together(
            part, value_z, kv_base, embed, embed_x, slide_out, out_x
        )
        part = lax.all_to_all(part, "tile", 0, 0, tiled=True)
        kv_z = [trade(kv_own, "tile", mask) for mask in (2, 4, 6)]
        wv_all = [value, value_z, value_y, trade(value_z, "tile", 1)]
    else:
        part = lax.psum(part, "tile")
        wv_all = [lax.all_gather(value, "tile", axis=0, tiled=True)]
    embed_all = [embed, trade(embed, "seg", 1), embed_x, trade(embed_x, "seg", 1)]
    slide_out_all = [slide_out, trade(slide_out, "seg", 1), out_x, trade(out_x, "seg", 1)]
    folded = call(
        fold_kernel,
        out_shape=sds((fresh, 8, round_up(cut, 128)), F32),
        in_specs=[VMEM] * 2,
        out_specs=VMEM,
        compiler_params=params(8 if small else 16),
        name="fold_key",
    )(part, vit_key)
    if small:
        kv_z = jnp.concatenate(kv_z, axis=0)
        folded, kv_z = together(folded, kv_z)
        folded = lax.all_to_all(folded, "tile", 0, 0, tiled=True)
        kv_all = [kv_own, kv_z, kv_y, trade(kv_z, "tile", 1)]
    else:
        folded = lax.all_to_all(folded, "tile", 0, 0, tiled=True)
        kv_all = [lax.all_gather(kv_base, "tile", axis=0, tiled=True)]

    sent = call(
        functools.partial(tile_kernel, cut),
        out_shape=sds((devices, 8, 256), F32),
        in_specs=[VMEM] * (6 + len(wv_all)),
        out_specs=VMEM,
        scratch_shapes=[
            pltpu.VMEM((8, DV), F32), pltpu.VMEM((tiles, 8, round_up(cut, 128)), F32),
        ],
        compiler_params=params(16 if small else 32),
        name="tile_attention",
    )(patches, vit_norm_gain, folded, layer_scale, embed_bias, vit_out, *wv_all)
    shares = lax.all_to_all(sent, ("tile", "seg"), 0, 0, tiled=True)

    block = min(total, 2048)
    steps = total // block
    kv_spec = pl.BlockSpec((block, 384), lambda i: (i, 0))
    krows_spec = pl.BlockSpec((24, block), lambda i: (0, i))
    kv_shape = [sds((total, 384), BF16)] if small else []
    *kv_sorted, krows, ml, acc = call(
        functools.partial(base_attention_kernel, span, total, padded),
        out_shape=(
            *kv_shape, sds((24, total), BF16),
            sds((3 * span, 128), F32), sds((3 * span, 256), F32),
        ),
        grid=(steps,),
        in_specs=[SMEM, SMEM, VMEM, VMEM] + ([VMEM] * 4 if small else [kv_spec]),
        out_specs=(*([kv_spec] if small else []), krows_spec, VMEM, VMEM),
        compiler_params=params(40),
        name="base_attention",
    )(slide_pos, offsets, pack, q_base, *kv_all)
    kv_sorted = kv_sorted[0] if small else kv_all[0]

    count = span // segs
    outs = call(
        functools.partial(fresh_kernel, span, total),
        out_shape=(sds((count, 256), BF16),) * 4 + (sds((count, DS), F32),),
        grid=(steps,),
        in_specs=[SMEM] * 2 + [VMEM] * 15 + [kv_spec, krows_spec],
        out_specs=(VMEM,) * 5,
        scratch_shapes=[
            pltpu.VMEM((padded, DS), F32),
            pltpu.VMEM((padded, 256), BF16),
            pltpu.VMEM((padded, 384), BF16),
            pltpu.VMEM((3 * padded, 128), F32),
            pltpu.VMEM((3 * padded, 256), F32),
            pltpu.VMEM((span, 256), F32),
        ],
        compiler_params=params(24 if small else 48),
        name="fresh_attention",
    )(
        slide_pos, offsets, pack, q_base, shares, final_gain, slide_gain, *weights, ml, acc,
        base_rows, *embed_all, kv_sorted, krows,
    )
    swapped = [outs[0]] + [trade(outs[mask], "seg", mask) for mask in range(1, 4)]
    return call(
        out_kernel,
        out_shape=sds((count, DS), BF16),
        in_specs=[VMEM] * 9,
        out_specs=VMEM,
        compiler_params=params(8),
        name="slide_next",
    )(outs[4], *swapped, *slide_out_all)


def solution(mesh):
    return jax.shard_map(
        shards,
        mesh=mesh,
        in_specs=(
            P("tile", None, None), P(), P("tile", "seg"), P("tile", "seg"), P("tile", "seg"),
            P("seg", None), P(), P(), P(None, "seg"), P("seg"), P(), P("tile", None), P("tile"),
            P(), P(), P(None, "seg"), P(None, "seg"), P(None, "seg"), P("seg", None), P(),
        ),
        out_specs=P(("tile", "seg"), None),
        check_vma=False,
    )
```

```python
import functools
import math

import jax
import jax.numpy as jnp
from jax import lax
from jax.experimental import pallas as pl
from jax.experimental.pallas import tpu as pltpu
from jax.sharding import PartitionSpec as P

DV = 1536
HV = 24
DS = 768
HS = 12
HEAD = 64

EPS = 1e-06
LOW = -1e30
F32 = jnp.float32
BF16 = jnp.bfloat16
I32 = jnp.int32
VMEM = pl.BlockSpec(memory_space=pltpu.VMEM)
SMEM = pl.BlockSpec(memory_space=pltpu.SMEM)
NT = (((1,), (1,)), ((), ()))
MIB = 1024 * 1024


def params(room):
    return pltpu.CompilerParams(vmem_limit_bytes=room * MIB)


def round_up(value, unit):
    return -(-value // unit) * unit


def layer_norm(values, scaling):
    center = values - jnp.mean(values, axis=-1, keepdims=True)
    spread = jnp.mean(center * center, axis=-1, keepdims=True)
    return center * lax.rsqrt(spread + EPS) * scaling


def dot(a, b):
    return jnp.dot(a, b, preferred_element_type=F32)


def dot_nt(a, b):
    return lax.dot_general(a, b, NT, preferred_element_type=F32)


def class_kernel(fresh, patch_ref, gain_ref, pos_ref, kept_ref, pack_ref):
    parts, _, width = pack_ref.shape
    cut = DV // parts
    rows = kept_ref.shape[0]
    row = patch_ref[0, 0:1].astype(F32)
    normed = layer_norm(row, gain_ref[...].reshape(1, DV)).astype(BF16).astype(F32)
    place = lax.broadcasted_iota(I32, (1, rows), 1) + lax.axis_index("tile") * rows
    kept = kept_ref[...].reshape(1, rows) != 0
    lane = lax.broadcasted_iota(I32, (1, width), 1)
    flags = jnp.zeros((1, width), F32)
    for index in range(fresh):
        hit = jnp.where((place == pos_ref[index]) & kept, 1.0, 0.0)
        flags = jnp.where(lane == index, jnp.max(hit, axis=1, keepdims=True), flags)
    for part in range(parts):
        pack_ref[part] = jnp.broadcast_to(flags, pack_ref.shape[1:])
        pack_ref[part, 0:1, 0:cut] = normed[:, part * cut : (part + 1) * cut]


def column(row, rows):
    width = row.shape[1]
    same = lax.broadcasted_iota(I32, (rows, width), 0) == lax.broadcasted_iota(
        I32, (rows, width), 1
    )
    return jnp.sum(jnp.where(same, row, 0.0), axis=1, keepdims=True)


def base_kernel(
    cached_ref, kept_ref, mask_ref, gain_ref, wq_ref, wk_ref, wv_ref, rows_ref, q_ref, kv_ref
):
    span = kept_ref.shape[0]
    kept = column(jnp.where(kept_ref[...].reshape(1, span) != 0, 1.0, 0.0), span)
    mask_row = mask_ref[...].reshape(1, DS).astype(BF16).astype(F32)
    rows = jnp.where(kept < 0.5, mask_row, cached_ref[...].astype(F32))
    rows_ref[...] = rows.astype(BF16)
    normed = layer_norm(rows, gain_ref[...].reshape(1, DS)).astype(BF16)
    project(normed, wq_ref, wk_ref, wv_ref, q_ref, kv_ref)


def project(normed, wq_ref, wk_ref, wv_ref, q_ref, kv_ref):
    q = dot_nt(normed, wq_ref[...]).astype(BF16) * BF16(1.0 / math.sqrt(HEAD))
    k = dot_nt(normed, wk_ref[...]).astype(BF16)
    v = dot_nt(normed, wv_ref[...]).astype(BF16)
    q_ref[:, 0:192] = q
    q_ref[:, 192:256] = jnp.zeros((q.shape[0], 64), BF16)
    kv_ref[:, 0:192] = k
    kv_ref[:, 192:256] = v[:, 128:192]
    kv_ref[:, 256:384] = v[:, 0:128]


def query_kernel(cut, pack_ref, wq_ref, part_ref):
    rows = pack_ref[:, 0, 0:cut].astype(BF16)
    part = dot(rows, wq_ref[...])
    if len(part_ref.shape) == 3:
        part_ref[...] = jnp.broadcast_to(part[None], part_ref.shape)
    else:
        part_ref[...] = part


def fold_kernel(part_ref, wk_ref, fold_ref):
    if len(part_ref.shape) == 3:
        queries = part_ref[0]
        for index in range(1, part_ref.shape[0]):
            queries = queries + part_ref[index]
    else:
        queries = part_ref[...]
    tiles, width = queries.shape
    queries = queries.astype(BF16).astype(F32)
    spread = jnp.broadcast_to(queries[:, None], (tiles, 8, width))
    head = lax.broadcasted_iota(I32, spread.shape, 1)
    lane = lax.broadcasted_iota(I32, spread.shape, 2)
    spread = jnp.where(lane // HEAD == head, spread, 0.0).reshape(tiles * 8, width).astype(BF16)
    cut = wk_ref.shape[0]
    result = dot_nt(spread, wk_ref[...]).reshape(tiles, 8, cut)
    fold_ref[:, :, 0:cut] = result
    if cut < fold_ref.shape[2]:
        fold_ref[:, :, cut:] = jnp.zeros((tiles, 8, fold_ref.shape[2] - cut), F32)


def token_kernel(patch_ref, gain_ref, normed_ref):
    tokens = patch_ref[0].astype(F32)
    normed_ref[...] = layer_norm(tokens, gain_ref[...].reshape(1, DV)).astype(BF16)


def tile_kernel(cut, patch_ref, normed_ref, fold_ref, scale_ref, bias_ref, wo_ref, *refs):
    *wv_refs, sent_ref, fold_s, mixed_s, share_s = refs
    parts = fold_ref.shape[0]
    for part in range(parts):
        fold_s[:, part * cut : (part + 1) * cut] = fold_ref[part, :, 0:cut]
    normed = normed_ref[...]
    scores = dot_nt(fold_s[...].astype(BF16), normed) * (1.0 / math.sqrt(HEAD))
    highest = jnp.max(scores, axis=-1, keepdims=True)
    exponent = jnp.exp(scores - highest)
    prob = (exponent / jnp.sum(exponent, axis=-1, keepdims=True)).astype(BF16)
    mixed = dot(prob, normed)
    if len(wv_refs) == 1:
        values = dot(mixed.astype(BF16), wv_refs[0][...])
    else:
        for part in range(parts):
            mixed_s[part, :, 0:cut] = mixed[:, part * cut : (part + 1) * cut]
        values = jnp.zeros((8, wo_ref.shape[0]), F32)
        me = lax.axis_index("tile")
        for masks, ref in zip(GROUPS, wv_refs):
            for index, mask in enumerate(masks):
                piece = mixed_s[me ^ mask][:, 0:cut].astype(BF16)
                values = values + dot(piece, ref[index * cut : (index + 1) * cut])
    head = lax.broadcasted_iota(I32, values.shape, 0)
    lane = lax.broadcasted_iota(I32, values.shape, 1)
    tmix = jnp.sum(jnp.where(lane // HEAD == head, values, 0.0), axis=0, keepdims=True)
    tmix = jnp.broadcast_to(tmix, (8, tmix.shape[1])).astype(BF16)
    share = dot(tmix, wo_ref[...])[0:1] * scale_ref[...].reshape(1, DV)
    class_token = patch_ref[0, 0:1].astype(F32)
    share = share + jnp.where(lax.axis_index("seg") == 0, class_token, 0.0)
    share_s[...] = jnp.zeros_like(share_s)
    for row in range(DV // 128):
        share_s[row : row + 1, :] = share[:, row * 128 : (row + 1) * 128]
    bias = bias_ref[...].reshape(1, 192)
    high = bias.astype(BF16).astype(F32)
    for row, term in ((12, high), (14, bias - high)):
        share_s[row : row + 1, :] = term[:, 0:128]
        share_s[row + 1 : row + 2, 0:64] = term[:, 128:192]
    sent_ref[...] = jnp.broadcast_to(share_s[...].astype(BF16)[None], sent_ref.shape)


def branch_rows(position, axis, offset_ref, span, total):
    shape = (1, 24) if axis == 1 else (24, 1)
    index = lax.broadcasted_iota(I32, shape, axis)
    branch = index % 8
    residue = jnp.full(shape, -1, I32)
    shift = jnp.zeros(shape, I32)
    for b in range(offset_ref.shape[0]):
        for head in range(3):
            offset = offset_ref[b, lax.axis_index("seg") * 3 + head]
            residue = jnp.where(index == head * 8 + b, offset, residue)
        length = min(2 * span * 4**b, total)
        shift = jnp.where(branch == b, length.bit_length() - 1, shift)
    below = jnp.left_shift(jnp.int32(1), branch) - 1
    mine = jnp.right_shift(jnp.zeros(shape, I32) + lax.axis_index("tile") * span, shift)
    return ((position & below) == residue) & (jnp.right_shift(position, shift) == mine)


def as_bf16(condition):
    return jnp.where(condition, 1.0, 0.0).astype(BF16)


def stack_heads(values, size):
    lane = lax.broadcasted_iota(I32, (1, values.shape[1]), 1)
    zero = jnp.zeros_like(values)
    return jnp.concatenate(
        [jnp.where(lane // size == head, values, zero) for head in range(3)], axis=0
    )


def attend(q, q_rows, kv_ref, k_rows):
    scores = dot_nt(q, kv_ref[:, 0:256])
    count = dot(q_rows, k_rows)
    scores = jnp.where(count > 0.5, scores, LOW)
    highest = jnp.max(scores, axis=-1, keepdims=True)
    weight = jnp.exp(scores - highest) * count
    denom = jnp.sum(weight, axis=-1, keepdims=True)
    numer = dot(weight.astype(BF16), kv_ref[:, 128:384])
    return highest, denom, numer


def merge(old, new):
    old_max, old_den, old_num = old
    new_max, new_den, new_num = new
    top = jnp.maximum(old_max, new_max)
    keep = jnp.exp(old_max - top)
    take = jnp.exp(new_max - top)
    return top, old_den * keep + new_den * take, old_num * keep + new_num * take


def clear_state(ml_ref, acc_ref):
    lane = lax.broadcasted_iota(I32, ml_ref.shape, 1)
    ml_ref[...] = jnp.where(lane < 8, LOW, 0.0)
    acc_ref[...] = jnp.zeros_like(acc_ref)


def add_state(new, head, ml_ref, acc_ref):
    old = ml_ref[:, head : head + 1], ml_ref[:, head + 8 : head + 9], acc_ref[...]
    top, den, num = merge(old, new)
    lane = lax.broadcasted_iota(I32, ml_ref.shape, 1)
    ml_ref[...] = jnp.where(lane == head, top, jnp.where(lane == head + 8, den, ml_ref[...]))
    acc_ref[...] = jnp.where(value_lanes(head), num, acc_ref[...])


def add_stacked(new, ml_ref, acc_ref):
    rows = acc_ref.shape[0]
    for head in range(3):
        add_state([x[head * rows : (head + 1) * rows] for x in new], head, ml_ref, acc_ref)


def value_lanes(head):
    return lax.broadcasted_iota(I32, (1, 256), 1) // HEAD == (2, 3, 1)[head]


def finish(ml_ref, acc_ref):
    result = jnp.zeros(acc_ref.shape, F32)
    for head in range(3):
        den = ml_ref[:, head + 8 : head + 9]
        den = jnp.where(den > 0.0, den, 1.0)
        result = jnp.where(value_lanes(head), acc_ref[...] / den, result)
    return result


def fresh_places(padded, pack_ref, pos_ref):
    flags = pack_ref[0, 1:2, :]
    for part in range(1, pack_ref.shape[0]):
        flags = flags + pack_ref[part, 1:2, :]
    flag_col = column(flags, padded)
    lane = lax.broadcasted_iota(I32, (1, padded), 1)
    sub = lax.broadcasted_iota(I32, (padded, 1), 0)
    row = jnp.full((1, padded), -1, I32)
    col = jnp.full((padded, 1), -1, I32)
    for index in range(pos_ref.shape[0]):
        row = jnp.where(lane == index, pos_ref[index], row)
        col = jnp.where(sub == index, pos_ref[index], col)
    return row, col, flags[:, 0:padded] > 0.5, flag_col > 0.5


def key_places(masks, block, span, step):
    place = lax.broadcasted_iota(I32, (1, block), 1)
    if masks is None:
        return place + step * block
    mask = jnp.zeros_like(place)
    for index, value in enumerate(masks):
        mask = jnp.where(place // span == index, value, mask)
    return (lax.axis_index("tile") ^ mask) * span + (place & (span - 1))


def key_rows(place, pos_col, flag_col, offset_ref, span, total):
    rows = branch_rows(place, 0, offset_ref, span, total)
    taken = jnp.where((place == pos_col) & flag_col, 1.0, 0.0)
    taken = jnp.max(taken, axis=0, keepdims=True)
    return as_bf16(rows & (taken < 0.5))


def base_attention_kernel(
    span, total, padded, groups, state, pos_ref, offset_ref, pack_ref, q_ref, *refs
):
    kv_refs, refs = refs[: len(groups)], refs[len(groups) :]
    ml_ref, acc_ref = refs[-2:]
    step = pl.program_id(0)
    rows = q_ref.shape[0]

    @pl.when(step == 0)
    def _():
        if state:
            ml_ref[...] = refs[0][...]
            acc_ref[...] = refs[1][...]
        else:
            clear_state(ml_ref, acc_ref)

    _, pos_col, _, flag_col = fresh_places(padded, pack_ref, pos_ref)
    place = lax.broadcasted_iota(I32, (rows, 1), 0) + lax.axis_index("tile") * span
    q_rows = as_bf16(branch_rows(place, 1, offset_ref, span, total))
    q = q_ref[...]
    lane = lax.broadcasted_iota(I32, (1, 256), 1)
    branch = lax.broadcasted_iota(I32, (1, 24), 1)
    for masks, kv_ref in zip(groups, kv_refs):
        keys = key_places(masks, kv_ref.shape[0], span, step)
        k_rows = key_rows(keys, pos_col, flag_col, offset_ref, span, total)
        for head in range(3):
            q_head = jnp.where(lane // HEAD == head, q, jnp.zeros_like(q))
            r_head = jnp.where(branch // 8 == head, q_rows, jnp.zeros_like(q_rows))
            add_state(attend(q_head, r_head, kv_ref, k_rows), head, ml_ref, acc_ref)


def fresh_kernel(
    span, total, groups, pos_ref, offset_ref, pack_ref, q_ref, shares_ref, final_ref, gain_ref,
    wq_ref, wk_ref, wv_ref, ml_ref, acc_ref, rows_ref, *refs,
):
    embed_refs, refs = refs[:4], refs[4:]
    kv_refs, refs = refs[: len(groups)], refs[len(groups) :]
    outs, refs = refs[:4], refs[4:]
    mine_ref, fresh_s, qf_s, kvf_s, mlf_s, accf_s, mlb_s, att_s = refs
    step = pl.program_id(0)
    rows = q_ref.shape[0]
    padded = fresh_s.shape[0]
    seg = lax.axis_index("seg")
    pos_row, pos_col, flag_row, flag_col = fresh_places(padded, pack_ref, pos_ref)
    f_rows = stack_heads(as_bf16(branch_rows(pos_col, 1, offset_ref, span, total)), 8)

    @pl.when(step == 0)
    def _():
        tiles = shares_ref.shape[0] // 4
        shares = shares_ref[...].astype(F32)
        bias = shares[0:4]
        summed = jnp.sum(shares.reshape(tiles, 4, 16, 128), axis=1)
        pooled = jnp.concatenate([summed[:, row, :] for row in range(DV // 128)], axis=1)
        summary = layer_norm(pooled, final_ref[...].reshape(1, DV)).astype(BF16)
        fresh_s[...] = jnp.zeros_like(fresh_s)
        pieces = [dot_nt(summary, ref[...]) for ref in embed_refs]
        for part in range(4):
            piece = pieces[0]
            for mask in range(1, 4):
                piece = jnp.where((seg ^ part) == mask, pieces[mask], piece)
            own = bias[part]
            own = own[12:14] + own[14:16]
            own = jnp.concatenate([own[0:1], own[1:2, 0:64]], axis=1)
            piece = (piece + own).astype(BF16).astype(F32)
            fresh_s[0:tiles, part * 192 : (part + 1) * 192] = piece
        normed = layer_norm(fresh_s[...], gain_ref[...].reshape(1, DS)).astype(BF16)
        project(normed, wq_ref, wk_ref, wv_ref, qf_s, kvf_s)
        clear_state(mlf_s, accf_s)

    qf = stack_heads(qf_s[...], HEAD)
    for masks, kv_ref in zip(groups, kv_refs):
        keys = key_places(masks, kv_ref.shape[0], span, step)
        k_rows = key_rows(keys, pos_col, flag_col, offset_ref, span, total)
        add_stacked(attend(qf, f_rows, kv_ref, k_rows), mlf_s, accf_s)

    @pl.when(step == pl.num_programs(0) - 1)
    def _():
        first = lax.axis_index("tile") * span
        place = lax.broadcasted_iota(I32, (rows, 1), 0) + first
        q_rows = stack_heads(as_bf16(branch_rows(place, 1, offset_ref, span, total)), 8)
        k_rows = as_bf16(branch_rows(pos_row, 0, offset_ref, span, total) & flag_row)
        mlb_s[...] = ml_ref[...]
        att_s[...] = acc_ref[...]
        add_stacked(attend(stack_heads(q_ref[...], HEAD), q_rows, kvf_s, k_rows), mlb_s, att_s)
        base = finish(mlb_s, att_s)
        add_stacked(attend(qf, f_rows, kvf_s, k_rows), mlf_s, accf_s)
        fresh = finish(mlf_s, accf_s)
        chosen = as_bf16((place == pos_row) & flag_row)
        hit = jnp.sum(chosen.astype(F32), axis=1, keepdims=True) > 0.5
        att_s[...] = jnp.where(hit, dot(chosen, fresh.astype(BF16)), base)
        count = rows // 4
        for mask in range(4):
            start = pl.multiple_of((seg ^ mask) * count, count)
            outs[mask][...] = att_s[pl.ds(start, count), :].astype(BF16)
        start = pl.multiple_of(seg * count, count)
        place = lax.broadcasted_iota(I32, (count, 1), 0) + first + start
        chosen = as_bf16((place == pos_row) & flag_row)
        hit = jnp.sum(chosen.astype(F32), axis=1, keepdims=True) > 0.5
        placed = dot(chosen, fresh_s[...].astype(BF16))
        old = rows_ref[pl.ds(start, count), :].astype(F32)
        mine_ref[...] = jnp.where(hit, placed, old)


def out_kernel(mine_ref, *refs):
    out_ref = refs[8]
    total = mine_ref[...]
    for mask in range(4):
        att, weight = refs[mask][...], refs[4 + mask]
        total = total + dot(att[:, 128:256], weight[0:128])
        total = total + dot(att[:, 64:128], weight[128:192])
    out_ref[...] = total.astype(BF16)


def trade(block, axis, mask):
    count = lax.axis_size(axis)
    return lax.ppermute(block, axis, [(i, i ^ mask) for i in range(count)])


GROUPS = ((0,), (2, 4, 6), (1,), (3, 5, 7))


def together(*values):
    return lax.optimization_barrier(values)


def shards(
    patches, vit_norm_gain, vit_query, vit_key, vit_value, vit_out, layer_scale, final_gain,
    embed_proj, embed_bias, slide_pos, cached, kept, mask_token, slide_gain, slide_query,
    slide_key, slide_value, slide_out, offsets,
):
    tiles = lax.axis_size("tile")
    segs = lax.axis_size("seg")
    devices = tiles * segs
    span = cached.shape[0]
    total = span * tiles
    cut, local_cols = vit_query.shape
    fresh = slide_pos.shape[0]
    padded = max(16, fresh)
    small = tiles == 8
    call = pl.pallas_call
    sds = jax.ShapeDtypeStruct
    weights = (slide_query.T, slide_key.T, slide_value.T)
    embed = embed_proj.T

    pack = call(
        functools.partial(class_kernel, fresh),
        out_shape=sds((tiles, 8, 256), F32),
        grid=(1,),
        in_specs=[pl.BlockSpec((1, 16, DV), lambda i: (0, 0, 0)), VMEM, SMEM, VMEM],
        out_specs=VMEM,
        compiler_params=params(60),
        name="class_row",
    )(patches, vit_norm_gain, slide_pos, kept)
    pack, cached = together(pack, cached)
    pack = lax.all_to_all(pack, "tile", 0, 0, tiled=True)
    base_rows, q_base, kv_base = call(
        base_kernel,
        out_shape=(sds((span, DS), BF16), sds((span, 256), BF16), sds((span, 384), BF16)),
        in_specs=[VMEM] * 7,
        out_specs=(VMEM,) * 3,
        compiler_params=params(16),
        name="base_rows",
    )(cached, kept, mask_token, slide_gain, *weights)
    value = vit_value
    if small:
        kv_base, value = together(kv_base, value)
        value_z = jnp.concatenate([trade(value, "tile", mask) for mask in GROUPS[1]], axis=0)
        value_y = trade(value, "tile", 1)
        kv_y = trade(kv_base, "tile", 1)

    part_shape = (tiles, fresh, local_cols) if small else (fresh, local_cols)
    part = call(
        functools.partial(query_kernel, cut),
        out_shape=sds(part_shape, F32),
        in_specs=[VMEM] * 2,
        out_specs=VMEM,
        compiler_params=params(8 if small else 16),
        name="query_share",
    )(pack, vit_query)
    part, patches = together(part, patches)
    if small:
        part = lax.all_to_all(part, "tile", 0, 0, tiled=True)
    else:
        part = lax.psum(part, "tile")
    normed = call(
        token_kernel,
        out_shape=sds(patches.shape[1:], BF16),
        in_specs=[VMEM] * 2,
        out_specs=VMEM,
        compiler_params=params(12),
        name="token_norm",
    )(patches, vit_norm_gain)
    if small:
        normed, value_z, kv_own = together(normed, value_z, kv_base)
        wv_all = [value, value_z, value_y, trade(value_z, "tile", 1)]
        kv_z = jnp.concatenate([trade(kv_own, "tile", mask) for mask in GROUPS[1]], axis=0)
    else:
        wv_all = [lax.all_gather(value, "tile", axis=0, tiled=True)]

    folded = call(
        fold_kernel,
        out_shape=sds((fresh, 8, round_up(cut, 128)), F32),
        in_specs=[VMEM] * 2,
        out_specs=VMEM,
        compiler_params=params(8 if small else 16),
        name="fold_key",
    )(part, vit_key)
    if small:
        folded, kv_z = together(folded, kv_z)
        kv_all = [kv_own, kv_z, kv_y, trade(kv_z, "tile", 1)]
        groups = GROUPS
    else:
        kv_all = [lax.all_gather(kv_base, "tile", axis=0, tiled=True)]
        groups = (None,)
    folded = lax.all_to_all(folded, "tile", 0, 0, tiled=True)
    block = min(total, 2048)
    steps = 1 if small else total // block
    kv_spec = VMEM if small else pl.BlockSpec((block, 384), lambda i: (i, 0))

    def attention(blocks, picked, state):
        return call(
            functools.partial(
                base_attention_kernel, span, total, padded, picked, len(state) > 0
            ),
            out_shape=(sds((span, 128), F32), sds((span, 256), F32)),
            grid=(steps,),
            in_specs=[SMEM, SMEM, VMEM, VMEM] + [kv_spec] * len(blocks) + [VMEM] * len(state),
            out_specs=(VMEM, VMEM),
            compiler_params=params(16 if small else 32),
            name="base_attention",
        )(slide_pos, offsets, pack, q_base, *blocks, *state)

    state = attention(kv_all[:2], groups[:2], ())
    state, embed, slide_out = together(state, embed, slide_out)
    embed_x = trade(embed, "seg", 2)
    out_x = trade(slide_out, "seg", 2)

    sent = call(
        functools.partial(tile_kernel, cut),
        out_shape=sds((devices, 16, 128), BF16),
        in_specs=[VMEM] * (6 + len(wv_all)),
        out_specs=VMEM,
        scratch_shapes=[
            pltpu.VMEM((8, DV), F32), pltpu.VMEM((tiles, 8, round_up(cut, 128)), F32),
            pltpu.VMEM((16, 128), F32),
        ],
        compiler_params=params(16 if small else 32),
        name="tile_attention",
    )(patches, normed, folded, layer_scale, embed_bias, vit_out, *wv_all)
    sent, state, embed_x, out_x = together(sent, state, embed_x, out_x)
    shares = lax.all_to_all(sent, ("tile", "seg"), 0, 0, tiled=True)
    if small:
        state = attention(kv_all[2:], groups[2:], state)
    embed_all = [embed, trade(embed, "seg", 1), embed_x, trade(embed_x, "seg", 1)]
    slide_out_all = [slide_out, trade(slide_out, "seg", 1), out_x, trade(out_x, "seg", 1)]

    count = span // segs
    outs = call(
        functools.partial(fresh_kernel, span, total, groups),
        out_shape=(sds((count, 256), BF16),) * 4 + (sds((count, DS), F32),),
        grid=(steps,),
        in_specs=[SMEM] * 2 + [VMEM] * 15 + [kv_spec] * len(kv_all),
        out_specs=(VMEM,) * 5,
        scratch_shapes=[
            pltpu.VMEM((padded, DS), F32),
            pltpu.VMEM((padded, 256), BF16),
            pltpu.VMEM((padded, 384), BF16),
            pltpu.VMEM((padded, 128), F32),
            pltpu.VMEM((padded, 256), F32),
            pltpu.VMEM((span, 128), F32),
            pltpu.VMEM((span, 256), F32),
        ],
        compiler_params=params(16 if small else 48),
        name="fresh_attention",
    )(
        slide_pos, offsets, pack, q_base, shares, final_gain, slide_gain, *weights, *state,
        base_rows, *embed_all, *kv_all,
    )
    swapped = [outs[0]] + [trade(outs[mask], "seg", mask) for mask in range(1, 4)]
    return call(
        out_kernel,
        out_shape=sds((count, DS), BF16),
        in_specs=[VMEM] * 9,
        out_specs=VMEM,
        compiler_params=params(8),
        name="slide_next",
    )(outs[4], *swapped, *slide_out_all)


def solution(mesh):
    return jax.shard_map(
        shards,
        mesh=mesh,
        in_specs=(
            P("tile", None, None), P(), P("tile", "seg"), P("tile", "seg"), P("tile", "seg"),
            P("seg", None), P(), P(), P(None, "seg"), P("seg"), P(), P("tile", None), P("tile"),
            P(), P(), P(None, "seg"), P(None, "seg"), P(None, "seg"), P("seg", None), P(),
        ),
        out_specs=P(("tile", "seg"), None),
        check_vma=False,
    )
```

```python
import functools
import math

import jax
import jax.numpy as jnp
from jax import lax
from jax.experimental import pallas as pl
from jax.experimental.pallas import tpu as pltpu
from jax.sharding import PartitionSpec as P

DV = 1536
HV = 24
DS = 768
HS = 12
HEAD = 64

EPS = 1e-06
LOW = -1e30
F32 = jnp.float32
BF16 = jnp.bfloat16
I32 = jnp.int32
VMEM = pl.BlockSpec(memory_space=pltpu.VMEM)
SMEM = pl.BlockSpec(memory_space=pltpu.SMEM)
NT = (((1,), (1,)), ((), ()))
MIB = 1024 * 1024


def params(room):
    return pltpu.CompilerParams(vmem_limit_bytes=room * MIB)


def round_up(value, unit):
    return -(-value // unit) * unit


def layer_norm(values, scaling):
    center = values - jnp.mean(values, axis=-1, keepdims=True)
    spread = jnp.mean(center * center, axis=-1, keepdims=True)
    return center * lax.rsqrt(spread + EPS) * scaling


def dot(a, b):
    return jnp.dot(a, b, preferred_element_type=F32)


def dot_nt(a, b):
    return lax.dot_general(a, b, NT, preferred_element_type=F32)


def class_kernel(fresh, patch_ref, gain_ref, pos_ref, kept_ref, pack_ref):
    parts, _, width = pack_ref.shape
    cut = DV // parts
    rows = kept_ref.shape[0]
    row = patch_ref[0, 0:1].astype(F32)
    normed = layer_norm(row, gain_ref[...].reshape(1, DV)).astype(BF16).astype(F32)
    place = lax.broadcasted_iota(I32, (1, rows), 1) + lax.axis_index("tile") * rows
    kept = kept_ref[...].reshape(1, rows) != 0
    lane = lax.broadcasted_iota(I32, (1, width), 1)
    flags = jnp.zeros((1, width), F32)
    for index in range(fresh):
        hit = jnp.where((place == pos_ref[index]) & kept, 1.0, 0.0)
        flags = jnp.where(lane == index, jnp.max(hit, axis=1, keepdims=True), flags)
    for part in range(parts):
        pack_ref[part] = jnp.broadcast_to(flags, pack_ref.shape[1:])
        pack_ref[part, 0:1, 0:cut] = normed[:, part * cut : (part + 1) * cut]


def column(row, rows):
    width = row.shape[1]
    same = lax.broadcasted_iota(I32, (rows, width), 0) == lax.broadcasted_iota(
        I32, (rows, width), 1
    )
    return jnp.sum(jnp.where(same, row, 0.0), axis=1, keepdims=True)


def base_kernel(
    cached_ref, kept_ref, mask_ref, gain_ref, wq_ref, wk_ref, wv_ref, embed_ref, project_ref,
    rows_ref, q_ref, kv_ref, joined_ref,
):
    joined_ref[:, 0:DV] = embed_ref[...]
    joined_ref[:, DV:] = project_ref[...]
    span = kept_ref.shape[0]
    kept = column(jnp.where(kept_ref[...].reshape(1, span) != 0, 1.0, 0.0), span)
    mask_row = mask_ref[...].reshape(1, DS).astype(BF16).astype(F32)
    rows = jnp.where(kept < 0.5, mask_row, cached_ref[...].astype(F32))
    rows_ref[...] = rows.astype(BF16)
    normed = layer_norm(rows, gain_ref[...].reshape(1, DS)).astype(BF16)
    project(normed, wq_ref, wk_ref, wv_ref, q_ref, kv_ref)


def project(normed, wq_ref, wk_ref, wv_ref, q_ref, kv_ref):
    q = dot_nt(normed, wq_ref[...]).astype(BF16) * BF16(1.0 / math.sqrt(HEAD))
    k = dot_nt(normed, wk_ref[...]).astype(BF16)
    v = dot_nt(normed, wv_ref[...]).astype(BF16)
    q_ref[:, 0:192] = q
    q_ref[:, 192:256] = jnp.zeros((q.shape[0], 64), BF16)
    kv_ref[:, 0:192] = k
    kv_ref[:, 192:256] = v[:, 128:192]
    kv_ref[:, 256:384] = v[:, 0:128]


def query_kernel(cut, pack_ref, wq_ref, part_ref):
    rows = pack_ref[:, 0, 0:cut].astype(BF16)
    part = dot(rows, wq_ref[...])
    if len(part_ref.shape) == 3:
        part_ref[...] = jnp.broadcast_to(part[None], part_ref.shape)
    else:
        part_ref[...] = part


def fold_kernel(part_ref, wk_ref, fold_ref):
    if len(part_ref.shape) == 3:
        queries = part_ref[0]
        for index in range(1, part_ref.shape[0]):
            queries = queries + part_ref[index]
    else:
        queries = part_ref[...]
    tiles, width = queries.shape
    queries = queries.astype(BF16).astype(F32)
    spread = jnp.broadcast_to(queries[:, None], (tiles, 8, width))
    head = lax.broadcasted_iota(I32, spread.shape, 1)
    lane = lax.broadcasted_iota(I32, spread.shape, 2)
    spread = jnp.where(lane // HEAD == head, spread, 0.0).reshape(tiles * 8, width).astype(BF16)
    cut = wk_ref.shape[0]
    result = dot_nt(spread, wk_ref[...]).reshape(tiles, 8, cut)
    fold_ref[:, :, 0:cut] = result
    if cut < fold_ref.shape[2]:
        fold_ref[:, :, cut:] = jnp.zeros((tiles, 8, fold_ref.shape[2] - cut), F32)


def token_kernel(patch_ref, gain_ref, normed_ref):
    tokens = patch_ref[0].astype(F32)
    normed_ref[...] = layer_norm(tokens, gain_ref[...].reshape(1, DV)).astype(BF16)


def tile_kernel(cut, patch_ref, normed_ref, fold_ref, scale_ref, bias_ref, wo_ref, *refs):
    *wv_refs, sent_ref, fold_s, mixed_s, share_s = refs
    parts = fold_ref.shape[0]
    for part in range(parts):
        fold_s[:, part * cut : (part + 1) * cut] = fold_ref[part, :, 0:cut]
    normed = normed_ref[...]
    scores = dot_nt(fold_s[...].astype(BF16), normed) * (1.0 / math.sqrt(HEAD))
    highest = jnp.max(scores, axis=-1, keepdims=True)
    exponent = jnp.exp(scores - highest)
    prob = (exponent / jnp.sum(exponent, axis=-1, keepdims=True)).astype(BF16)
    mixed = dot(prob, normed)
    if len(wv_refs) == 1:
        values = dot(mixed.astype(BF16), wv_refs[0][...])
    else:
        for part in range(parts):
            mixed_s[part, :, 0:cut] = mixed[:, part * cut : (part + 1) * cut]
        values = jnp.zeros((8, wo_ref.shape[0]), F32)
        me = lax.axis_index("tile")
        for masks, ref in zip(GROUPS, wv_refs):
            for index, mask in enumerate(masks):
                piece = mixed_s[me ^ mask][:, 0:cut].astype(BF16)
                values = values + dot(piece, ref[index * cut : (index + 1) * cut])
    head = lax.broadcasted_iota(I32, values.shape, 0)
    lane = lax.broadcasted_iota(I32, values.shape, 1)
    tmix = jnp.sum(jnp.where(lane // HEAD == head, values, 0.0), axis=0, keepdims=True)
    tmix = jnp.broadcast_to(tmix, (8, tmix.shape[1])).astype(BF16)
    share = dot(tmix, wo_ref[...])[0:1] * scale_ref[...].reshape(1, DV)
    class_token = patch_ref[0, 0:1].astype(F32)
    share = share + jnp.where(lax.axis_index("seg") == 0, class_token, 0.0)
    share_s[...] = jnp.zeros_like(share_s)
    for row in range(DV // 128):
        share_s[row : row + 1, :] = share[:, row * 128 : (row + 1) * 128]
    bias = bias_ref[...].reshape(1, 192)
    high = bias.astype(BF16).astype(F32)
    for row, term in ((12, high), (14, bias - high)):
        share_s[row : row + 1, :] = term[:, 0:128]
        share_s[row + 1 : row + 2, 0:64] = term[:, 128:192]
    sent_ref[...] = jnp.broadcast_to(share_s[...].astype(BF16)[None], sent_ref.shape)


def branch_rows(position, axis, offset_ref, span, total):
    shape = (1, 24) if axis == 1 else (24, 1)
    index = lax.broadcasted_iota(I32, shape, axis)
    branch = index % 8
    residue = jnp.full(shape, -1, I32)
    shift = jnp.zeros(shape, I32)
    for b in range(offset_ref.shape[0]):
        for head in range(3):
            offset = offset_ref[b, lax.axis_index("seg") * 3 + head]
            residue = jnp.where(index == head * 8 + b, offset, residue)
        length = min(2 * span * 4**b, total)
        shift = jnp.where(branch == b, length.bit_length() - 1, shift)
    below = jnp.left_shift(jnp.int32(1), branch) - 1
    mine = jnp.right_shift(jnp.zeros(shape, I32) + lax.axis_index("tile") * span, shift)
    return ((position & below) == residue) & (jnp.right_shift(position, shift) == mine)


def as_bf16(condition):
    return jnp.where(condition, 1.0, 0.0).astype(BF16)


def stack_heads(values, size):
    lane = lax.broadcasted_iota(I32, (1, values.shape[1]), 1)
    zero = jnp.zeros_like(values)
    return jnp.concatenate(
        [jnp.where(lane // size == head, values, zero) for head in range(3)], axis=0
    )


def attend(q, q_rows, kv_ref, k_rows):
    scores = dot_nt(q, kv_ref[:, 0:256])
    count = dot(q_rows, k_rows)
    scores = jnp.where(count > 0.5, scores, LOW)
    highest = jnp.max(scores, axis=-1, keepdims=True)
    weight = jnp.exp(scores - highest) * count
    denom = jnp.sum(weight, axis=-1, keepdims=True)
    numer = dot(weight.astype(BF16), kv_ref[:, 128:384])
    return highest, denom, numer


def merge(old, new):
    old_max, old_den, old_num = old
    new_max, new_den, new_num = new
    top = jnp.maximum(old_max, new_max)
    keep = jnp.exp(old_max - top)
    take = jnp.exp(new_max - top)
    return top, old_den * keep + new_den * take, old_num * keep + new_num * take


def clear_state(ml_ref, acc_ref):
    lane = lax.broadcasted_iota(I32, ml_ref.shape, 1)
    ml_ref[...] = jnp.where(lane < 8, LOW, 0.0)
    acc_ref[...] = jnp.zeros_like(acc_ref)


def add_state(new, head, ml_ref, acc_ref):
    old = ml_ref[:, head : head + 1], ml_ref[:, head + 8 : head + 9], acc_ref[...]
    top, den, num = merge(old, new)
    lane = lax.broadcasted_iota(I32, ml_ref.shape, 1)
    ml_ref[...] = jnp.where(lane == head, top, jnp.where(lane == head + 8, den, ml_ref[...]))
    acc_ref[...] = jnp.where(value_lanes(head), num, acc_ref[...])


def add_stacked(new, ml_ref, acc_ref):
    rows = acc_ref.shape[0]
    for head in range(3):
        add_state([x[head * rows : (head + 1) * rows] for x in new], head, ml_ref, acc_ref)


def value_lanes(head):
    return lax.broadcasted_iota(I32, (1, 256), 1) // HEAD == (2, 3, 1)[head]


def finish(ml_ref, acc_ref):
    result = jnp.zeros(acc_ref.shape, F32)
    for head in range(3):
        den = ml_ref[:, head + 8 : head + 9]
        den = jnp.where(den > 0.0, den, 1.0)
        result = jnp.where(value_lanes(head), acc_ref[...] / den, result)
    return result


def fresh_places(padded, pack_ref, pos_ref):
    flags = pack_ref[0, 1:2, :]
    for part in range(1, pack_ref.shape[0]):
        flags = flags + pack_ref[part, 1:2, :]
    flag_col = column(flags, padded)
    lane = lax.broadcasted_iota(I32, (1, padded), 1)
    sub = lax.broadcasted_iota(I32, (padded, 1), 0)
    row = jnp.full((1, padded), -1, I32)
    col = jnp.full((padded, 1), -1, I32)
    for index in range(pos_ref.shape[0]):
        row = jnp.where(lane == index, pos_ref[index], row)
        col = jnp.where(sub == index, pos_ref[index], col)
    return row, col, flags[:, 0:padded] > 0.5, flag_col > 0.5


def key_places(masks, block, span, step):
    place = lax.broadcasted_iota(I32, (1, block), 1)
    if masks is None:
        return place + step * block
    mask = jnp.zeros_like(place)
    for index, value in enumerate(masks):
        mask = jnp.where(place // span == index, value, mask)
    return (lax.axis_index("tile") ^ mask) * span + (place & (span - 1))


def key_rows(place, pos_col, flag_col, offset_ref, span, total):
    rows = branch_rows(place, 0, offset_ref, span, total)
    taken = jnp.where((place == pos_col) & flag_col, 1.0, 0.0)
    taken = jnp.max(taken, axis=0, keepdims=True)
    return as_bf16(rows & (taken < 0.5))


def base_attention_kernel(
    span, total, padded, groups, pos_ref, offset_ref, pack_ref, q_ref, *refs
):
    kv_refs, refs = refs[: len(groups)], refs[len(groups) :]
    kv_ref = kv_refs[0] if len(groups) == 1 else refs[0]
    krows_ref, ml_ref, acc_ref = refs[-3:]
    step = pl.program_id(0)
    rows = q_ref.shape[0]

    @pl.when(step == 0)
    def _():
        clear_state(ml_ref, acc_ref)

    masks = None
    if len(groups) > 1:
        masks = sum(groups, ())
        start = 0
        for ref in kv_refs:
            kv_ref[start : start + ref.shape[0], :] = ref[...]
            start += ref.shape[0]
    _, pos_col, _, flag_col = fresh_places(padded, pack_ref, pos_ref)
    place = lax.broadcasted_iota(I32, (rows, 1), 0) + lax.axis_index("tile") * span
    q_rows = stack_heads(as_bf16(branch_rows(place, 1, offset_ref, span, total)), 8)
    keys = key_places(masks, kv_ref.shape[0], span, step)
    k_rows = key_rows(keys, pos_col, flag_col, offset_ref, span, total)
    krows_ref[...] = k_rows
    add_stacked(attend(stack_heads(q_ref[...], HEAD), q_rows, kv_ref, k_rows), ml_ref, acc_ref)


def fresh_kernel(
    span, total, pos_ref, offset_ref, pack_ref, q_ref, shares_ref, final_ref, gain_ref,
    wq_ref, wk_ref, wv_ref, ml_ref, acc_ref, rows_ref, *refs,
):
    embed_refs, refs = refs[:4], refs[4:]
    kv_ref, krows_ref, *refs = refs
    outs, refs = refs[:4], refs[4:]
    mine_ref, fresh_s, qf_s, kvf_s, mlf_s, accf_s, mlb_s, att_s = refs
    step = pl.program_id(0)
    rows = q_ref.shape[0]
    padded = fresh_s.shape[0]
    seg = lax.axis_index("seg")
    pos_row, pos_col, flag_row, flag_col = fresh_places(padded, pack_ref, pos_ref)
    f_rows = stack_heads(as_bf16(branch_rows(pos_col, 1, offset_ref, span, total)), 8)

    @pl.when(step == 0)
    def _():
        tiles = shares_ref.shape[0] // 4
        shares = shares_ref[...].astype(F32)
        bias = shares[0:4]
        summed = jnp.sum(shares.reshape(tiles, 4, 16, 128), axis=1)
        pooled = jnp.concatenate([summed[:, row, :] for row in range(DV // 128)], axis=1)
        summary = layer_norm(pooled, final_ref[...].reshape(1, DV)).astype(BF16)
        fresh_s[...] = jnp.zeros_like(fresh_s)
        pieces = [dot_nt(summary, ref[:, 0:DV]) for ref in embed_refs]
        for part in range(4):
            piece = pieces[0]
            for mask in range(1, 4):
                piece = jnp.where((seg ^ part) == mask, pieces[mask], piece)
            own = bias[part]
            own = own[12:14] + own[14:16]
            own = jnp.concatenate([own[0:1], own[1:2, 0:64]], axis=1)
            piece = (piece + own).astype(BF16).astype(F32)
            fresh_s[0:tiles, part * 192 : (part + 1) * 192] = piece
        normed = layer_norm(fresh_s[...], gain_ref[...].reshape(1, DS)).astype(BF16)
        project(normed, wq_ref, wk_ref, wv_ref, qf_s, kvf_s)
        clear_state(mlf_s, accf_s)

    qf = stack_heads(qf_s[...], HEAD)
    add_stacked(attend(qf, f_rows, kv_ref, krows_ref[...]), mlf_s, accf_s)

    @pl.when(step == pl.num_programs(0) - 1)
    def _():
        first = lax.axis_index("tile") * span
        place = lax.broadcasted_iota(I32, (rows, 1), 0) + first
        q_rows = stack_heads(as_bf16(branch_rows(place, 1, offset_ref, span, total)), 8)
        k_rows = as_bf16(branch_rows(pos_row, 0, offset_ref, span, total) & flag_row)
        mlb_s[...] = ml_ref[...]
        att_s[...] = acc_ref[...]
        add_stacked(attend(stack_heads(q_ref[...], HEAD), q_rows, kvf_s, k_rows), mlb_s, att_s)
        base = finish(mlb_s, att_s)
        add_stacked(attend(qf, f_rows, kvf_s, k_rows), mlf_s, accf_s)
        fresh = finish(mlf_s, accf_s)
        chosen = as_bf16((place == pos_row) & flag_row)
        hit = jnp.sum(chosen.astype(F32), axis=1, keepdims=True) > 0.5
        att_s[...] = jnp.where(hit, dot(chosen, fresh.astype(BF16)), base)
        count = rows // 4
        for mask in range(4):
            start = pl.multiple_of((seg ^ mask) * count, count)
            outs[mask][...] = att_s[pl.ds(start, count), :].astype(BF16)
        start = pl.multiple_of(seg * count, count)
        place = lax.broadcasted_iota(I32, (count, 1), 0) + first + start
        chosen = as_bf16((place == pos_row) & flag_row)
        hit = jnp.sum(chosen.astype(F32), axis=1, keepdims=True) > 0.5
        placed = dot(chosen, fresh_s[...].astype(BF16))
        old = rows_ref[pl.ds(start, count), :].astype(F32)
        mine_ref[...] = jnp.where(hit, placed, old)


def out_kernel(mine_ref, *refs):
    out_ref = refs[8]
    total = mine_ref[...]
    for mask in range(4):
        att, weight = refs[mask][...], refs[4 + mask][...]
        total = total + dot(att[:, 128:256], weight[0:128])
        total = total + dot(att[:, 64:128], weight[128:192])
    out_ref[...] = total.astype(BF16)


def trade(block, axis, mask):
    count = lax.axis_size(axis)
    return lax.ppermute(block, axis, [(i, i ^ mask) for i in range(count)])


GROUPS = ((0,), (2, 4, 6), (1,), (3, 5, 7))


def together(*values):
    return lax.optimization_barrier(values)


def shards(
    patches, vit_norm_gain, vit_query, vit_key, vit_value, vit_out, layer_scale, final_gain,
    embed_proj, embed_bias, slide_pos, cached, kept, mask_token, slide_gain, slide_query,
    slide_key, slide_value, slide_out, offsets,
):
    tiles = lax.axis_size("tile")
    segs = lax.axis_size("seg")
    devices = tiles * segs
    span = cached.shape[0]
    total = span * tiles
    cut, local_cols = vit_query.shape
    fresh = slide_pos.shape[0]
    padded = max(16, fresh)
    small = tiles == 8
    call = pl.pallas_call
    sds = jax.ShapeDtypeStruct
    weights = (slide_query.T, slide_key.T, slide_value.T)
    embed = embed_proj.T

    pack = call(
        functools.partial(class_kernel, fresh),
        out_shape=sds((tiles, 8, 256), F32),
        grid=(1,),
        in_specs=[pl.BlockSpec((1, 16, DV), lambda i: (0, 0, 0)), VMEM, SMEM, VMEM],
        out_specs=VMEM,
        compiler_params=params(60),
        name="class_row",
    )(patches, vit_norm_gain, slide_pos, kept)
    pack, value, cached = together(pack, vit_value, cached)
    pack = lax.all_to_all(pack, "tile", 0, 0, tiled=True)
    base_rows, q_base, kv_base, joined = call(
        base_kernel,
        out_shape=(
            sds((span, DS), BF16), sds((span, 256), BF16), sds((span, 384), BF16),
            sds((192, DV + DS), BF16),
        ),
        in_specs=[VMEM] * 9,
        out_specs=(VMEM,) * 4,
        compiler_params=params(60),
        name="base_rows",
    )(cached, kept, mask_token, slide_gain, *weights, embed, slide_out)
    joined_x = trade(joined, "seg", 2)
    if small:
        value_z = jnp.concatenate([trade(value, "tile", mask) for mask in GROUPS[1]], axis=0)
        value_y = trade(value, "tile", 1)
        kv_y = trade(kv_base, "tile", 1)

    part_shape = (tiles, fresh, local_cols) if small else (fresh, local_cols)
    part = call(
        functools.partial(query_kernel, cut),
        out_shape=sds(part_shape, F32),
        in_specs=[VMEM] * 2,
        out_specs=VMEM,
        compiler_params=params(8 if small else 16),
        name="query_share",
    )(pack, vit_query)
    if small:
        part, value_z, kv_own = together(part, value_z, kv_base)
        part = lax.all_to_all(part, "tile", 0, 0, tiled=True)
    else:
        part = lax.psum(part, "tile")
    normed = call(
        token_kernel,
        out_shape=sds(patches.shape[1:], BF16),
        in_specs=[VMEM] * 2,
        out_specs=VMEM,
        compiler_params=params(12),
        name="token_norm",
    )(patches, vit_norm_gain)
    joined, joined_x = together(joined, joined_x)
    joined_all = [joined, trade(joined, "seg", 1), joined_x, trade(joined_x, "seg", 1)]
    if small:
        wv_all = [value, value_z, value_y, trade(value_z, "tile", 1)]
        kv_z = jnp.concatenate([trade(kv_own, "tile", mask) for mask in GROUPS[1]], axis=0)
    else:
        wv_all = [lax.all_gather(value, "tile", axis=0, tiled=True)]

    folded = call(
        fold_kernel,
        out_shape=sds((fresh, 8, round_up(cut, 128)), F32),
        in_specs=[VMEM] * 2,
        out_specs=VMEM,
        compiler_params=params(8 if small else 16),
        name="fold_key",
    )(part, vit_key)
    if small:
        folded, kv_z, kv_y = together(folded, kv_z, kv_y)
        kv_all = [kv_own, kv_z, kv_y, trade(kv_z, "tile", 1)]
        groups = GROUPS
    else:
        kv_all = [lax.all_gather(kv_base, "tile", axis=0, tiled=True)]
        groups = (None,)
    folded = lax.all_to_all(folded, "tile", 0, 0, tiled=True)
    sent = call(
        functools.partial(tile_kernel, cut),
        out_shape=sds((devices, 16, 128), BF16),
        in_specs=[VMEM] * (6 + len(wv_all)),
        out_specs=VMEM,
        scratch_shapes=[
            pltpu.VMEM((8, DV), F32), pltpu.VMEM((tiles, 8, round_up(cut, 128)), F32),
            pltpu.VMEM((16, 128), F32),
        ],
        compiler_params=params(16 if small else 32),
        name="tile_attention",
    )(patches, normed, folded, layer_scale, embed_bias, vit_out, *wv_all)
    shares = lax.all_to_all(sent, ("tile", "seg"), 0, 0, tiled=True)
    block = min(total, 2048)
    steps = total // block
    kv_spec = pl.BlockSpec((block, 384), lambda i: (i, 0))
    krows_spec = pl.BlockSpec((24, block), lambda i: (0, i))
    kv_shape = [sds((total, 384), BF16)] if small else []
    *kv_sorted, krows, ml, acc = call(
        functools.partial(base_attention_kernel, span, total, padded, groups),
        out_shape=(
            *kv_shape, sds((24, total), BF16), sds((span, 128), F32), sds((span, 256), F32),
        ),
        grid=(steps,),
        in_specs=[SMEM, SMEM, VMEM, VMEM] + ([VMEM] * 4 if small else [kv_spec]),
        out_specs=(*([kv_spec] if small else []), krows_spec, VMEM, VMEM),
        compiler_params=params(60),
        name="base_attention",
    )(slide_pos, offsets, pack, q_base, *kv_all)
    kv_sorted = kv_sorted[0] if small else kv_all[0]

    count = span // segs
    outs = call(
        functools.partial(fresh_kernel, span, total),
        out_shape=(sds((count, 256), BF16),) * 4 + (sds((count, DS), F32),),
        grid=(steps,),
        in_specs=[SMEM] * 2 + [VMEM] * 9 + [VMEM] * 2
        + [pl.BlockSpec((192, DV), lambda i: (0, 0))] * 4 + [kv_spec, krows_spec],
        out_specs=(VMEM,) * 5,
        scratch_shapes=[
            pltpu.VMEM((padded, DS), F32),
            pltpu.VMEM((padded, 256), BF16),
            pltpu.VMEM((padded, 384), BF16),
            pltpu.VMEM((padded, 128), F32),
            pltpu.VMEM((padded, 256), F32),
            pltpu.VMEM((span, 128), F32),
            pltpu.VMEM((span, 256), F32),
        ],
        compiler_params=params(60),
        name="fresh_attention",
    )(
        slide_pos, offsets, pack, q_base, shares, final_gain, slide_gain, *weights, ml, acc,
        base_rows, *joined_all, kv_sorted, krows,
    )
    swapped = [outs[0]] + [trade(outs[mask], "seg", mask) for mask in range(1, 4)]
    return call(
        out_kernel,
        out_shape=sds((count, DS), BF16),
        grid=(1,),
        in_specs=[VMEM] * 5 + [pl.BlockSpec((192, DS), lambda i: (0, DV // DS))] * 4,
        out_specs=VMEM,
        compiler_params=params(60),
        name="slide_next",
    )(outs[4], *swapped, *joined_all)


def solution(mesh):
    return jax.shard_map(
        shards,
        mesh=mesh,
        in_specs=(
            P("tile", None, None), P(), P("tile", "seg"), P("tile", "seg"), P("tile", "seg"),
            P("seg", None), P(), P(), P(None, "seg"), P("seg"), P(), P("tile", None), P("tile"),
            P(), P(), P(None, "seg"), P(None, "seg"), P(None, "seg"), P("seg", None), P(),
        ),
        out_specs=P(("tile", "seg"), None),
        check_vma=False,
    )
```

```python
import functools
import math

import jax
import jax.numpy as jnp
from jax import lax
from jax.experimental import pallas as pl
from jax.experimental.pallas import tpu as pltpu
from jax.sharding import PartitionSpec as P

DV = 1536
HV = 24
DS = 768
HS = 12
HEAD = 64

EPS = 1e-06
LOW = -1e30
F32 = jnp.float32
BF16 = jnp.bfloat16
I32 = jnp.int32
VMEM = pl.BlockSpec(memory_space=pltpu.VMEM)
SMEM = pl.BlockSpec(memory_space=pltpu.SMEM)
ANY = pl.BlockSpec(memory_space=pl.ANY)
NT = (((1,), (1,)), ((), ()))
MIB = 1024 * 1024


def params(room):
    return pltpu.CompilerParams(vmem_limit_bytes=room * MIB)


def round_up(value, unit):
    return -(-value // unit) * unit


def layer_norm(values, scaling):
    center = values - jnp.mean(values, axis=-1, keepdims=True)
    spread = jnp.mean(center * center, axis=-1, keepdims=True)
    return center * lax.rsqrt(spread + EPS) * scaling


def dot(a, b):
    return jnp.dot(a, b, preferred_element_type=F32)


def dot_nt(a, b):
    return lax.dot_general(a, b, NT, preferred_element_type=F32)


def class_kernel(fresh, patch_ref, gain_ref, pos_ref, kept_ref, pack_ref):
    parts, _, width = pack_ref.shape
    cut = DV // parts
    rows = kept_ref.shape[0]
    row = patch_ref[0, 0:1].astype(F32)
    normed = layer_norm(row, gain_ref[...].reshape(1, DV)).astype(BF16).astype(F32)
    place = lax.broadcasted_iota(I32, (1, rows), 1) + lax.axis_index("tile") * rows
    kept = kept_ref[...].reshape(1, rows) != 0
    lane = lax.broadcasted_iota(I32, (1, width), 1)
    flags = jnp.zeros((1, width), F32)
    for index in range(fresh):
        hit = jnp.where((place == pos_ref[index]) & kept, 1.0, 0.0)
        flags = jnp.where(lane == index, jnp.max(hit, axis=1, keepdims=True), flags)
    for part in range(parts):
        pack_ref[part] = jnp.broadcast_to(flags, pack_ref.shape[1:])
        pack_ref[part, 0:1, 0:cut] = normed[:, part * cut : (part + 1) * cut]


def column(row, rows):
    width = row.shape[1]
    same = lax.broadcasted_iota(I32, (rows, width), 0) == lax.broadcasted_iota(
        I32, (rows, width), 1
    )
    return jnp.sum(jnp.where(same, row, 0.0), axis=1, keepdims=True)


def base_kernel(
    cached_ref, kept_ref, mask_ref, gain_ref, wq_ref, wk_ref, wv_ref, embed_ref, project_ref,
    rows_ref, q_ref, kv_ref, joined_ref,
):
    joined_ref[:, 0:DV] = embed_ref[...]
    joined_ref[:, DV:] = project_ref[...]
    span = kept_ref.shape[0]
    kept = column(jnp.where(kept_ref[...].reshape(1, span) != 0, 1.0, 0.0), span)
    mask_row = mask_ref[...].reshape(1, DS).astype(BF16).astype(F32)
    rows = jnp.where(kept < 0.5, mask_row, cached_ref[...].astype(F32))
    rows_ref[...] = rows.astype(BF16)
    normed = layer_norm(rows, gain_ref[...].reshape(1, DS)).astype(BF16)
    project(normed, wq_ref, wk_ref, wv_ref, q_ref, kv_ref)


def project(normed, wq_ref, wk_ref, wv_ref, q_ref, kv_ref):
    q = dot_nt(normed, wq_ref[...]).astype(BF16) * BF16(1.0 / math.sqrt(HEAD))
    k = dot_nt(normed, wk_ref[...]).astype(BF16)
    v = dot_nt(normed, wv_ref[...]).astype(BF16)
    q_ref[:, 0:192] = q
    q_ref[:, 192:256] = jnp.zeros((q.shape[0], 64), BF16)
    kv_ref[:, 0:192] = k
    kv_ref[:, 192:256] = v[:, 128:192]
    kv_ref[:, 256:384] = v[:, 0:128]


def query_kernel(cut, pack_ref, wq_ref, *refs):
    part_ref = refs[-1]
    rows = pack_ref[:, 0, 0:cut].astype(BF16)
    part = dot(rows, wq_ref[...])
    if len(part_ref.shape) == 3:
        part_ref[...] = jnp.broadcast_to(part[None], part_ref.shape)
    else:
        part_ref[...] = part


def fold_kernel(part_ref, wk_ref, *refs):
    fold_ref = refs[-1]
    if len(part_ref.shape) == 3:
        queries = part_ref[0]
        for index in range(1, part_ref.shape[0]):
            queries = queries + part_ref[index]
    else:
        queries = part_ref[...]
    tiles, width = queries.shape
    queries = queries.astype(BF16).astype(F32)
    spread = jnp.broadcast_to(queries[:, None], (tiles, 8, width))
    head = lax.broadcasted_iota(I32, spread.shape, 1)
    lane = lax.broadcasted_iota(I32, spread.shape, 2)
    spread = jnp.where(lane // HEAD == head, spread, 0.0).reshape(tiles * 8, width).astype(BF16)
    cut = wk_ref.shape[0]
    result = dot_nt(spread, wk_ref[...]).reshape(tiles, 8, cut)
    fold_ref[:, :, 0:cut] = result
    if cut < fold_ref.shape[2]:
        fold_ref[:, :, cut:] = jnp.zeros((tiles, 8, fold_ref.shape[2] - cut), F32)


def gate_kernel(*refs):
    del refs


def token_kernel(patch_ref, gain_ref, normed_ref):
    tokens = patch_ref[0].astype(F32)
    normed_ref[...] = layer_norm(tokens, gain_ref[...].reshape(1, DV)).astype(BF16)


def tile_kernel(cut, patch_ref, normed_ref, fold_ref, scale_ref, bias_ref, wo_ref, *refs):
    *wv_refs, sent_ref, fold_s, mixed_s, share_s = refs
    parts = fold_ref.shape[0]
    for part in range(parts):
        fold_s[:, part * cut : (part + 1) * cut] = fold_ref[part, :, 0:cut]
    normed = normed_ref[...]
    scores = dot_nt(fold_s[...].astype(BF16), normed) * (1.0 / math.sqrt(HEAD))
    highest = jnp.max(scores, axis=-1, keepdims=True)
    exponent = jnp.exp(scores - highest)
    prob = (exponent / jnp.sum(exponent, axis=-1, keepdims=True)).astype(BF16)
    mixed = dot(prob, normed)
    if len(wv_refs) == 1:
        values = dot(mixed.astype(BF16), wv_refs[0][...])
    else:
        for part in range(parts):
            mixed_s[part, :, 0:cut] = mixed[:, part * cut : (part + 1) * cut]
        values = jnp.zeros((8, wo_ref.shape[0]), F32)
        me = lax.axis_index("tile")
        for masks, ref in zip(GROUPS, wv_refs):
            for index, mask in enumerate(masks):
                piece = mixed_s[me ^ mask][:, 0:cut].astype(BF16)
                values = values + dot(piece, ref[index * cut : (index + 1) * cut])
    head = lax.broadcasted_iota(I32, values.shape, 0)
    lane = lax.broadcasted_iota(I32, values.shape, 1)
    tmix = jnp.sum(jnp.where(lane // HEAD == head, values, 0.0), axis=0, keepdims=True)
    tmix = jnp.broadcast_to(tmix, (8, tmix.shape[1])).astype(BF16)
    share = dot(tmix, wo_ref[...])[0:1] * scale_ref[...].reshape(1, DV)
    class_token = patch_ref[0, 0:1].astype(F32)
    share = share + jnp.where(lax.axis_index("seg") == 0, class_token, 0.0)
    share_s[...] = jnp.zeros_like(share_s)
    for row in range(DV // 128):
        share_s[row : row + 1, :] = share[:, row * 128 : (row + 1) * 128]
    bias = bias_ref[...].reshape(1, 192)
    high = bias.astype(BF16).astype(F32)
    for row, term in ((12, high), (14, bias - high)):
        share_s[row : row + 1, :] = term[:, 0:128]
        share_s[row + 1 : row + 2, 0:64] = term[:, 128:192]
    sent_ref[...] = jnp.broadcast_to(share_s[...].astype(BF16)[None], sent_ref.shape)


def branch_rows(position, axis, offset_ref, span, total):
    shape = (1, 24) if axis == 1 else (24, 1)
    index = lax.broadcasted_iota(I32, shape, axis)
    branch = index % 8
    residue = jnp.full(shape, -1, I32)
    shift = jnp.zeros(shape, I32)
    for b in range(offset_ref.shape[0]):
        for head in range(3):
            offset = offset_ref[b, lax.axis_index("seg") * 3 + head]
            residue = jnp.where(index == head * 8 + b, offset, residue)
        length = min(2 * span * 4**b, total)
        shift = jnp.where(branch == b, length.bit_length() - 1, shift)
    below = jnp.left_shift(jnp.int32(1), branch) - 1
    mine = jnp.right_shift(jnp.zeros(shape, I32) + lax.axis_index("tile") * span, shift)
    return ((position & below) == residue) & (jnp.right_shift(position, shift) == mine)


def as_bf16(condition):
    return jnp.where(condition, 1.0, 0.0).astype(BF16)


def stack_heads(values, size):
    lane = lax.broadcasted_iota(I32, (1, values.shape[1]), 1)
    zero = jnp.zeros_like(values)
    return jnp.concatenate(
        [jnp.where(lane // size == head, values, zero) for head in range(3)], axis=0
    )


def attend(q, q_rows, kv_ref, k_rows):
    scores = dot_nt(q, kv_ref[:, 0:256])
    count = dot(q_rows, k_rows)
    scores = jnp.where(count > 0.5, scores, LOW)
    highest = jnp.max(scores, axis=-1, keepdims=True)
    weight = jnp.exp(scores - highest) * count
    denom = jnp.sum(weight, axis=-1, keepdims=True)
    numer = dot(weight.astype(BF16), kv_ref[:, 128:384])
    return highest, denom, numer


def merge(old, new):
    old_max, old_den, old_num = old
    new_max, new_den, new_num = new
    top = jnp.maximum(old_max, new_max)
    keep = jnp.exp(old_max - top)
    take = jnp.exp(new_max - top)
    return top, old_den * keep + new_den * take, old_num * keep + new_num * take


def clear_state(ml_ref, acc_ref):
    lane = lax.broadcasted_iota(I32, ml_ref.shape, 1)
    ml_ref[...] = jnp.where(lane < 8, LOW, 0.0)
    acc_ref[...] = jnp.zeros_like(acc_ref)


def add_state(new, head, ml_ref, acc_ref):
    old = ml_ref[:, head : head + 1], ml_ref[:, head + 8 : head + 9], acc_ref[...]
    top, den, num = merge(old, new)
    lane = lax.broadcasted_iota(I32, ml_ref.shape, 1)
    ml_ref[...] = jnp.where(lane == head, top, jnp.where(lane == head + 8, den, ml_ref[...]))
    acc_ref[...] = jnp.where(value_lanes(head), num, acc_ref[...])


def add_stacked(new, ml_ref, acc_ref):
    rows = acc_ref.shape[0]
    for head in range(3):
        add_state([x[head * rows : (head + 1) * rows] for x in new], head, ml_ref, acc_ref)


def value_lanes(head):
    return lax.broadcasted_iota(I32, (1, 256), 1) // HEAD == (2, 3, 1)[head]


def finish(ml_ref, acc_ref):
    result = jnp.zeros(acc_ref.shape, F32)
    for head in range(3):
        den = ml_ref[:, head + 8 : head + 9]
        den = jnp.where(den > 0.0, den, 1.0)
        result = jnp.where(value_lanes(head), acc_ref[...] / den, result)
    return result


def fresh_places(padded, pack_ref, pos_ref):
    flags = pack_ref[0, 1:2, :]
    for part in range(1, pack_ref.shape[0]):
        flags = flags + pack_ref[part, 1:2, :]
    flag_col = column(flags, padded)
    lane = lax.broadcasted_iota(I32, (1, padded), 1)
    sub = lax.broadcasted_iota(I32, (padded, 1), 0)
    row = jnp.full((1, padded), -1, I32)
    col = jnp.full((padded, 1), -1, I32)
    for index in range(pos_ref.shape[0]):
        row = jnp.where(lane == index, pos_ref[index], row)
        col = jnp.where(sub == index, pos_ref[index], col)
    return row, col, flags[:, 0:padded] > 0.5, flag_col > 0.5


def key_places(masks, block, span, step):
    place = lax.broadcasted_iota(I32, (1, block), 1)
    if masks is None:
        return place + step * block
    mask = jnp.zeros_like(place)
    for index, value in enumerate(masks):
        mask = jnp.where(place // span == index, value, mask)
    return (lax.axis_index("tile") ^ mask) * span + (place & (span - 1))


def key_rows(place, pos_col, flag_col, offset_ref, span, total):
    rows = branch_rows(place, 0, offset_ref, span, total)
    taken = jnp.where((place == pos_col) & flag_col, 1.0, 0.0)
    taken = jnp.max(taken, axis=0, keepdims=True)
    return as_bf16(rows & (taken < 0.5))


def base_attention_kernel(
    span, total, padded, groups, pos_ref, offset_ref, pack_ref, q_ref, *refs
):
    kv_refs, refs = refs[: len(groups)], refs[len(groups) :]
    kv_ref = kv_refs[0] if len(groups) == 1 else refs[0]
    krows_ref, ml_ref, acc_ref = refs[-3:]
    step = pl.program_id(0)
    rows = q_ref.shape[0]

    @pl.when(step == 0)
    def _():
        clear_state(ml_ref, acc_ref)

    masks = None
    if len(groups) > 1:
        masks = sum(groups, ())
        start = 0
        for ref in kv_refs:
            kv_ref[start : start + ref.shape[0], :] = ref[...]
            start += ref.shape[0]
    _, pos_col, _, flag_col = fresh_places(padded, pack_ref, pos_ref)
    place = lax.broadcasted_iota(I32, (rows, 1), 0) + lax.axis_index("tile") * span
    q_rows = stack_heads(as_bf16(branch_rows(place, 1, offset_ref, span, total)), 8)
    keys = key_places(masks, kv_ref.shape[0], span, step)
    k_rows = key_rows(keys, pos_col, flag_col, offset_ref, span, total)
    krows_ref[...] = k_rows
    add_stacked(attend(stack_heads(q_ref[...], HEAD), q_rows, kv_ref, k_rows), ml_ref, acc_ref)


def fresh_kernel(
    span, total, pos_ref, offset_ref, pack_ref, q_ref, shares_ref, final_ref, gain_ref,
    wq_ref, wk_ref, wv_ref, ml_ref, acc_ref, rows_ref, *refs,
):
    embed_refs, refs = refs[:4], refs[4:]
    kv_ref, krows_ref, *refs = refs
    outs, refs = refs[:4], refs[4:]
    mine_ref, fresh_s, qf_s, kvf_s, mlf_s, accf_s, mlb_s, att_s = refs
    step = pl.program_id(0)
    rows = q_ref.shape[0]
    padded = fresh_s.shape[0]
    seg = lax.axis_index("seg")
    pos_row, pos_col, flag_row, flag_col = fresh_places(padded, pack_ref, pos_ref)
    f_rows = stack_heads(as_bf16(branch_rows(pos_col, 1, offset_ref, span, total)), 8)

    @pl.when(step == 0)
    def _():
        tiles = shares_ref.shape[0] // 4
        shares = shares_ref[...].astype(F32)
        bias = shares[0:4]
        summed = jnp.sum(shares.reshape(tiles, 4, 16, 128), axis=1)
        pooled = jnp.concatenate([summed[:, row, :] for row in range(DV // 128)], axis=1)
        summary = layer_norm(pooled, final_ref[...].reshape(1, DV)).astype(BF16)
        fresh_s[...] = jnp.zeros_like(fresh_s)
        pieces = [dot_nt(summary, ref[:, 0:DV]) for ref in embed_refs]
        for part in range(4):
            piece = pieces[0]
            for mask in range(1, 4):
                piece = jnp.where((seg ^ part) == mask, pieces[mask], piece)
            own = bias[part]
            own = own[12:14] + own[14:16]
            own = jnp.concatenate([own[0:1], own[1:2, 0:64]], axis=1)
            piece = (piece + own).astype(BF16).astype(F32)
            fresh_s[0:tiles, part * 192 : (part + 1) * 192] = piece
        normed = layer_norm(fresh_s[...], gain_ref[...].reshape(1, DS)).astype(BF16)
        project(normed, wq_ref, wk_ref, wv_ref, qf_s, kvf_s)
        clear_state(mlf_s, accf_s)

    qf = stack_heads(qf_s[...], HEAD)
    add_stacked(attend(qf, f_rows, kv_ref, krows_ref[...]), mlf_s, accf_s)

    @pl.when(step == pl.num_programs(0) - 1)
    def _():
        first = lax.axis_index("tile") * span
        place = lax.broadcasted_iota(I32, (rows, 1), 0) + first
        q_rows = stack_heads(as_bf16(branch_rows(place, 1, offset_ref, span, total)), 8)
        k_rows = as_bf16(branch_rows(pos_row, 0, offset_ref, span, total) & flag_row)
        mlb_s[...] = ml_ref[...]
        att_s[...] = acc_ref[...]
        add_stacked(attend(stack_heads(q_ref[...], HEAD), q_rows, kvf_s, k_rows), mlb_s, att_s)
        base = finish(mlb_s, att_s)
        add_stacked(attend(qf, f_rows, kvf_s, k_rows), mlf_s, accf_s)
        fresh = finish(mlf_s, accf_s)
        chosen = as_bf16((place == pos_row) & flag_row)
        hit = jnp.sum(chosen.astype(F32), axis=1, keepdims=True) > 0.5
        att_s[...] = jnp.where(hit, dot(chosen, fresh.astype(BF16)), base)
        count = rows // 4
        for mask in range(4):
            start = pl.multiple_of((seg ^ mask) * count, count)
            outs[mask][...] = att_s[pl.ds(start, count), :].astype(BF16)
        start = pl.multiple_of(seg * count, count)
        place = lax.broadcasted_iota(I32, (count, 1), 0) + first + start
        chosen = as_bf16((place == pos_row) & flag_row)
        hit = jnp.sum(chosen.astype(F32), axis=1, keepdims=True) > 0.5
        placed = dot(chosen, fresh_s[...].astype(BF16))
        old = rows_ref[pl.ds(start, count), :].astype(F32)
        mine_ref[...] = jnp.where(hit, placed, old)


def out_kernel(mine_ref, *refs):
    out_ref = refs[8]
    total = mine_ref[...]
    for mask in range(4):
        att, weight = refs[mask][...], refs[4 + mask][...]
        total = total + dot(att[:, 128:256], weight[0:128])
        total = total + dot(att[:, 64:128], weight[128:192])
    out_ref[...] = total.astype(BF16)


def trade(block, axis, mask):
    count = lax.axis_size(axis)
    return lax.ppermute(block, axis, [(i, i ^ mask) for i in range(count)])


GROUPS = ((0,), (2, 4, 6), (1,), (3, 5, 7))


def together(*values):
    return lax.optimization_barrier(values)


def shards(
    patches, vit_norm_gain, vit_query, vit_key, vit_value, vit_out, layer_scale, final_gain,
    embed_proj, embed_bias, slide_pos, cached, kept, mask_token, slide_gain, slide_query,
    slide_key, slide_value, slide_out, offsets,
):
    tiles = lax.axis_size("tile")
    segs = lax.axis_size("seg")
    devices = tiles * segs
    span = cached.shape[0]
    total = span * tiles
    cut, local_cols = vit_query.shape
    fresh = slide_pos.shape[0]
    padded = max(16, fresh)
    small = tiles == 8
    call = pl.pallas_call
    sds = jax.ShapeDtypeStruct
    weights = (slide_query.T, slide_key.T, slide_value.T)
    embed = embed_proj.T

    pack = call(
        functools.partial(class_kernel, fresh),
        out_shape=sds((tiles, 8, 256), F32),
        grid=(1,),
        in_specs=[pl.BlockSpec((1, 16, DV), lambda i: (0, 0, 0)), VMEM, SMEM, VMEM],
        out_specs=VMEM,
        compiler_params=params(60),
        name="class_row",
    )(patches, vit_norm_gain, slide_pos, kept)
    pack, value, cached = together(pack, vit_value, cached)
    pack = lax.all_to_all(pack, "tile", 0, 0, tiled=True)
    base_rows, q_base, kv_base, joined = call(
        base_kernel,
        out_shape=(
            sds((span, DS), BF16), sds((span, 256), BF16), sds((span, 384), BF16),
            sds((192, DV + DS), BF16),
        ),
        in_specs=[VMEM] * 9,
        out_specs=(VMEM,) * 4,
        compiler_params=params(60),
        name="base_rows",
    )(cached, kept, mask_token, slide_gain, *weights, embed, slide_out)
    joined_x = trade(joined, "seg", 2)
    if small:
        value_z = jnp.concatenate([trade(value, "tile", mask) for mask in GROUPS[1]], axis=0)
        value_y = trade(value, "tile", 1)
        kv_y = trade(kv_base, "tile", 1)

    due = [value_y] if small else []
    part_shape = (tiles, fresh, local_cols) if small else (fresh, local_cols)
    part = call(
        functools.partial(query_kernel, cut),
        out_shape=sds(part_shape, F32),
        in_specs=[VMEM] * 2 + [ANY] * len(due),
        out_specs=VMEM,
        compiler_params=params(8 if small else 16),
        name="query_share",
    )(pack, vit_query, *due)
    if small:
        part, value_z, kv_own = together(part, value_z, kv_base)
        part = lax.all_to_all(part, "tile", 0, 0, tiled=True)
    else:
        part = lax.psum(part, "tile")
    normed = call(
        token_kernel,
        out_shape=sds(patches.shape[1:], BF16),
        in_specs=[VMEM] * 2,
        out_specs=VMEM,
        compiler_params=params(12),
        name="token_norm",
    )(patches, vit_norm_gain)
    joined, joined_x = together(joined, joined_x)
    joined_all = [joined, trade(joined, "seg", 1), joined_x, trade(joined_x, "seg", 1)]
    if small:
        wv_all = [value, value_z, value_y, trade(value_z, "tile", 1)]
        kv_z = jnp.concatenate([trade(kv_own, "tile", mask) for mask in GROUPS[1]], axis=0)
    else:
        wv_all = [lax.all_gather(value, "tile", axis=0, tiled=True)]

    due = [kv_y, wv_all[3]] if small else []
    folded = call(
        fold_kernel,
        out_shape=sds((fresh, 8, round_up(cut, 128)), F32),
        in_specs=[VMEM] * 2 + [ANY] * len(due),
        out_specs=VMEM,
        compiler_params=params(8 if small else 16),
        name="fold_key",
    )(part, vit_key, *due)
    if small:
        groups = GROUPS
    else:
        kv_all = [lax.all_gather(kv_base, "tile", axis=0, tiled=True)]
        groups = (None,)
    folded = lax.all_to_all(folded, "tile", 0, 0, tiled=True)
    if small:
        kv_z = call(
            gate_kernel,
            out_shape=sds(kv_z.shape, kv_z.dtype),
            in_specs=[ANY] * 2,
            out_specs=ANY,
            input_output_aliases={0: 0},
            compiler_params=params(8),
            name="third_over",
        )(kv_z, folded)
        kv_all = [kv_own, kv_z, kv_y, trade(kv_z, "tile", 1)]
    sent = call(
        functools.partial(tile_kernel, cut),
        out_shape=sds((devices, 16, 128), BF16),
        grid=(1,),
        in_specs=[pl.BlockSpec((1, 16, DV), lambda i: (0, 0, 0))] + [VMEM] * (5 + len(wv_all)),
        out_specs=VMEM,
        scratch_shapes=[
            pltpu.VMEM((8, DV), F32), pltpu.VMEM((tiles, 8, round_up(cut, 128)), F32),
            pltpu.VMEM((16, 128), F32),
        ],
        compiler_params=params(60),
        name="tile_attention",
    )(patches, normed, folded, layer_scale, embed_bias, vit_out, *wv_all)
    shares = lax.all_to_all(sent, ("tile", "seg"), 0, 0, tiled=True)
    block = min(total, 2048)
    steps = total // block
    kv_spec = pl.BlockSpec((block, 384), lambda i: (i, 0))
    krows_spec = pl.BlockSpec((24, block), lambda i: (0, i))
    kv_shape = [sds((total, 384), BF16)] if small else []
    *kv_sorted, krows, ml, acc = call(
        functools.partial(base_attention_kernel, span, total, padded, groups),
        out_shape=(
            *kv_shape, sds((24, total), BF16), sds((span, 128), F32), sds((span, 256), F32),
        ),
        grid=(steps,),
        in_specs=[SMEM, SMEM, VMEM, VMEM] + ([VMEM] * 4 if small else [kv_spec]),
        out_specs=(*([kv_spec] if small else []), krows_spec, VMEM, VMEM),
        compiler_params=params(60),
        name="base_attention",
    )(slide_pos, offsets, pack, q_base, *kv_all)
    kv_sorted = kv_sorted[0] if small else kv_all[0]

    count = span // segs
    outs = call(
        functools.partial(fresh_kernel, span, total),
        out_shape=(sds((count, 256), BF16),) * 4 + (sds((count, DS), F32),),
        grid=(steps,),
        in_specs=[SMEM] * 2 + [VMEM] * 9 + [VMEM] * 2
        + [pl.BlockSpec((192, DV), lambda i: (0, 0))] * 4 + [kv_spec, krows_spec],
        out_specs=(VMEM,) * 5,
        scratch_shapes=[
            pltpu.VMEM((padded, DS), F32),
            pltpu.VMEM((padded, 256), BF16),
            pltpu.VMEM((padded, 384), BF16),
            pltpu.VMEM((padded, 128), F32),
            pltpu.VMEM((padded, 256), F32),
            pltpu.VMEM((span, 128), F32),
            pltpu.VMEM((span, 256), F32),
        ],
        compiler_params=params(60),
        name="fresh_attention",
    )(
        slide_pos, offsets, pack, q_base, shares, final_gain, slide_gain, *weights, ml, acc,
        base_rows, *joined_all, kv_sorted, krows,
    )
    swapped = [outs[0]] + [trade(outs[mask], "seg", mask) for mask in range(1, 4)]
    return call(
        out_kernel,
        out_shape=sds((count, DS), BF16),
        grid=(1,),
        in_specs=[VMEM] * 5 + [pl.BlockSpec((192, DS), lambda i: (0, DV // DS))] * 4,
        out_specs=VMEM,
        compiler_params=params(60),
        name="slide_next",
    )(outs[4], *swapped, *joined_all)


def solution(mesh):
    return jax.shard_map(
        shards,
        mesh=mesh,
        in_specs=(
            P("tile", None, None), P(), P("tile", "seg"), P("tile", "seg"), P("tile", "seg"),
            P("seg", None), P(), P(), P(None, "seg"), P("seg"), P(), P("tile", None), P("tile"),
            P(), P(), P(None, "seg"), P(None, "seg"), P(None, "seg"), P("seg", None), P(),
        ),
        out_specs=P(("tile", "seg"), None),
        check_vma=False,
    )
```

```python
import functools
import math

import jax
import jax.numpy as jnp
from jax import lax
from jax.experimental import pallas as pl
from jax.experimental.pallas import tpu as pltpu
from jax.sharding import PartitionSpec as P

DV = 1536
HV = 24
DS = 768
HS = 12
HEAD = 64

EPS = 1e-06
LOW = -1e30
F32 = jnp.float32
BF16 = jnp.bfloat16
I32 = jnp.int32
VMEM = pl.BlockSpec(memory_space=pltpu.VMEM)
SMEM = pl.BlockSpec(memory_space=pltpu.SMEM)
ANY = pl.BlockSpec(memory_space=pl.ANY)
NT = (((1,), (1,)), ((), ()))
MIB = 1024 * 1024


def params(room):
    return pltpu.CompilerParams(vmem_limit_bytes=room * MIB)


def round_up(value, unit):
    return -(-value // unit) * unit


def layer_norm(values, scaling):
    center = values - jnp.mean(values, axis=-1, keepdims=True)
    spread = jnp.mean(center * center, axis=-1, keepdims=True)
    return center * lax.rsqrt(spread + EPS) * scaling


def dot(a, b):
    return jnp.dot(a, b, preferred_element_type=F32)


def dot_nt(a, b):
    return lax.dot_general(a, b, NT, preferred_element_type=F32)


def class_kernel(fresh, patch_ref, gain_ref, pos_ref, kept_ref, pack_ref):
    parts, _, width = pack_ref.shape
    cut = DV // parts
    rows = kept_ref.shape[0]
    row = patch_ref[0, 0:1].astype(F32)
    normed = layer_norm(row, gain_ref[...].reshape(1, DV)).astype(BF16).astype(F32)
    place = lax.broadcasted_iota(I32, (1, rows), 1) + lax.axis_index("tile") * rows
    kept = kept_ref[...].reshape(1, rows) != 0
    lane = lax.broadcasted_iota(I32, (1, width), 1)
    flags = jnp.zeros((1, width), F32)
    for index in range(fresh):
        hit = jnp.where((place == pos_ref[index]) & kept, 1.0, 0.0)
        flags = jnp.where(lane == index, jnp.max(hit, axis=1, keepdims=True), flags)
    for part in range(parts):
        pack_ref[part] = jnp.broadcast_to(flags, pack_ref.shape[1:])
        pack_ref[part, 0:1, 0:cut] = normed[:, part * cut : (part + 1) * cut]


def column(row, rows):
    width = row.shape[1]
    same = lax.broadcasted_iota(I32, (rows, width), 0) == lax.broadcasted_iota(
        I32, (rows, width), 1
    )
    return jnp.sum(jnp.where(same, row, 0.0), axis=1, keepdims=True)


def base_kernel(
    cached_ref, kept_ref, mask_ref, gain_ref, wq_ref, wk_ref, wv_ref, embed_ref, project_ref,
    rows_ref, q_ref, kv_ref, joined_ref,
):
    joined_ref[:, 0:DV] = embed_ref[...]
    joined_ref[:, DV:] = project_ref[...]
    span = kept_ref.shape[0]
    kept = column(jnp.where(kept_ref[...].reshape(1, span) != 0, 1.0, 0.0), span)
    mask_row = mask_ref[...].reshape(1, DS).astype(BF16).astype(F32)
    rows = jnp.where(kept < 0.5, mask_row, cached_ref[...].astype(F32))
    rows_ref[...] = rows.astype(BF16)
    normed = layer_norm(rows, gain_ref[...].reshape(1, DS)).astype(BF16)
    project(normed, wq_ref, wk_ref, wv_ref, q_ref, kv_ref)


def project(normed, wq_ref, wk_ref, wv_ref, q_ref, kv_ref):
    q = dot_nt(normed, wq_ref[...]).astype(BF16) * BF16(1.0 / math.sqrt(HEAD))
    k = dot_nt(normed, wk_ref[...]).astype(BF16)
    v = dot_nt(normed, wv_ref[...]).astype(BF16)
    q_ref[:, 0:192] = q
    q_ref[:, 192:256] = jnp.zeros((q.shape[0], 64), BF16)
    kv_ref[:, 0:192] = k
    kv_ref[:, 192:256] = v[:, 128:192]
    kv_ref[:, 256:384] = v[:, 0:128]


def query_kernel(cut, pack_ref, wq_ref, *refs):
    part_ref = refs[-1]
    rows = pack_ref[:, 0, 0:cut].astype(BF16)
    part = dot(rows, wq_ref[...])
    if len(part_ref.shape) == 3:
        part_ref[...] = jnp.broadcast_to(part[None], part_ref.shape)
    else:
        part_ref[...] = part


def fold_kernel(part_ref, wk_ref, *refs):
    fold_ref = refs[-1]
    if len(part_ref.shape) == 3:
        queries = part_ref[0]
        for index in range(1, part_ref.shape[0]):
            queries = queries + part_ref[index]
    else:
        queries = part_ref[...]
    tiles, width = queries.shape
    queries = queries.astype(BF16).astype(F32)
    spread = jnp.broadcast_to(queries[:, None], (tiles, 8, width))
    head = lax.broadcasted_iota(I32, spread.shape, 1)
    lane = lax.broadcasted_iota(I32, spread.shape, 2)
    spread = jnp.where(lane // HEAD == head, spread, 0.0).reshape(tiles * 8, width).astype(BF16)
    cut = wk_ref.shape[0]
    result = dot_nt(spread, wk_ref[...]).reshape(tiles, 8, cut)
    fold_ref[:, :, 0:cut] = result
    if cut < fold_ref.shape[2]:
        fold_ref[:, :, cut:] = jnp.zeros((tiles, 8, fold_ref.shape[2] - cut), F32)


def gate_kernel(*refs):
    del refs


def token_kernel(patch_ref, gain_ref, normed_ref):
    tokens = patch_ref[0].astype(F32)
    normed_ref[...] = layer_norm(tokens, gain_ref[...].reshape(1, DV)).astype(BF16)


def tile_kernel(cut, patch_ref, normed_ref, fold_ref, scale_ref, bias_ref, wo_ref, *refs):
    *wv_refs, sent_ref, fold_s, mixed_s, share_s = refs
    parts = fold_ref.shape[0]
    for part in range(parts):
        fold_s[:, part * cut : (part + 1) * cut] = fold_ref[part, :, 0:cut]
    normed = normed_ref[...]
    scores = dot_nt(fold_s[...].astype(BF16), normed) * (1.0 / math.sqrt(HEAD))
    highest = jnp.max(scores, axis=-1, keepdims=True)
    exponent = jnp.exp(scores - highest)
    prob = (exponent / jnp.sum(exponent, axis=-1, keepdims=True)).astype(BF16)
    mixed = dot(prob, normed)
    if len(wv_refs) == 1:
        values = dot(mixed.astype(BF16), wv_refs[0][...])
    else:
        for part in range(parts):
            mixed_s[part, :, 0:cut] = mixed[:, part * cut : (part + 1) * cut]
        values = jnp.zeros((8, wo_ref.shape[0]), F32)
        me = lax.axis_index("tile")
        for masks, ref in zip(GROUPS, wv_refs):
            for index, mask in enumerate(masks):
                piece = mixed_s[me ^ mask][:, 0:cut].astype(BF16)
                values = values + dot(piece, ref[index * cut : (index + 1) * cut])
    head = lax.broadcasted_iota(I32, values.shape, 0)
    lane = lax.broadcasted_iota(I32, values.shape, 1)
    tmix = jnp.sum(jnp.where(lane // HEAD == head, values, 0.0), axis=0, keepdims=True)
    tmix = jnp.broadcast_to(tmix, (8, tmix.shape[1])).astype(BF16)
    share = dot(tmix, wo_ref[...])[0:1] * scale_ref[...].reshape(1, DV)
    class_token = patch_ref[0, 0:1].astype(F32)
    share = share + jnp.where(lax.axis_index("seg") == 0, class_token, 0.0)
    share_s[...] = jnp.zeros_like(share_s)
    for row in range(DV // 128):
        share_s[row : row + 1, :] = share[:, row * 128 : (row + 1) * 128]
    bias = bias_ref[...].reshape(1, 192)
    high = bias.astype(BF16).astype(F32)
    for row, term in ((12, high), (14, bias - high)):
        share_s[row : row + 1, :] = term[:, 0:128]
        share_s[row + 1 : row + 2, 0:64] = term[:, 128:192]
    sent_ref[...] = jnp.broadcast_to(share_s[...].astype(BF16)[None], sent_ref.shape)


def branch_rows(position, axis, offset_ref, span, total):
    shape = (1, 24) if axis == 1 else (24, 1)
    index = lax.broadcasted_iota(I32, shape, axis)
    branch = index % 8
    residue = jnp.full(shape, -1, I32)
    shift = jnp.zeros(shape, I32)
    for b in range(offset_ref.shape[0]):
        for head in range(3):
            offset = offset_ref[b, lax.axis_index("seg") * 3 + head]
            residue = jnp.where(index == head * 8 + b, offset, residue)
        length = min(2 * span * 4**b, total)
        shift = jnp.where(branch == b, length.bit_length() - 1, shift)
    below = jnp.left_shift(jnp.int32(1), branch) - 1
    mine = jnp.right_shift(jnp.zeros(shape, I32) + lax.axis_index("tile") * span, shift)
    return ((position & below) == residue) & (jnp.right_shift(position, shift) == mine)


def as_bf16(condition):
    return jnp.where(condition, 1.0, 0.0).astype(BF16)


def stack_heads(values, size):
    lane = lax.broadcasted_iota(I32, (1, values.shape[1]), 1)
    zero = jnp.zeros_like(values)
    return jnp.concatenate(
        [jnp.where(lane // size == head, values, zero) for head in range(3)], axis=0
    )


def attend(q, q_rows, kv_ref, k_rows):
    scores = dot_nt(q, kv_ref[:, 0:256])
    count = dot(q_rows, k_rows)
    scores = jnp.where(count > 0.5, scores, LOW)
    highest = jnp.max(scores, axis=-1, keepdims=True)
    weight = jnp.exp(scores - highest) * count
    denom = jnp.sum(weight, axis=-1, keepdims=True)
    numer = dot(weight.astype(BF16), kv_ref[:, 128:384])
    return highest, denom, numer


def merge(old, new):
    old_max, old_den, old_num = old
    new_max, new_den, new_num = new
    top = jnp.maximum(old_max, new_max)
    keep = jnp.exp(old_max - top)
    take = jnp.exp(new_max - top)
    return top, old_den * keep + new_den * take, old_num * keep + new_num * take


def clear_state(ml_ref, acc_ref):
    lane = lax.broadcasted_iota(I32, ml_ref.shape, 1)
    ml_ref[...] = jnp.where(lane < 8, LOW, 0.0)
    acc_ref[...] = jnp.zeros_like(acc_ref)


def add_state(new, head, ml_ref, acc_ref):
    old = ml_ref[:, head : head + 1], ml_ref[:, head + 8 : head + 9], acc_ref[...]
    top, den, num = merge(old, new)
    lane = lax.broadcasted_iota(I32, ml_ref.shape, 1)
    ml_ref[...] = jnp.where(lane == head, top, jnp.where(lane == head + 8, den, ml_ref[...]))
    acc_ref[...] = jnp.where(value_lanes(head), num, acc_ref[...])


def set_stacked(new, ml_ref, acc_ref):
    rows = acc_ref.shape[0]
    lane = lax.broadcasted_iota(I32, ml_ref.shape, 1)
    ml = jnp.zeros(ml_ref.shape, F32)
    acc = jnp.zeros(acc_ref.shape, F32)
    for head in range(3):
        top, den, num = (x[head * rows : (head + 1) * rows] for x in new)
        ml = jnp.where(lane == head, top, jnp.where(lane == head + 8, den, ml))
        acc = jnp.where(value_lanes(head), num, acc)
    ml_ref[...] = ml
    acc_ref[...] = acc


def add_stacked(new, ml_ref, acc_ref):
    rows = acc_ref.shape[0]
    for head in range(3):
        add_state([x[head * rows : (head + 1) * rows] for x in new], head, ml_ref, acc_ref)


def value_lanes(head):
    return lax.broadcasted_iota(I32, (1, 256), 1) // HEAD == (2, 3, 1)[head]


def finish(ml_ref, acc_ref):
    result = jnp.zeros(acc_ref.shape, F32)
    for head in range(3):
        den = ml_ref[:, head + 8 : head + 9]
        den = jnp.where(den > 0.0, den, 1.0)
        result = jnp.where(value_lanes(head), acc_ref[...] / den, result)
    return result


def fresh_places(padded, pack_ref, pos_ref):
    flags = pack_ref[0, 1:2, :]
    for part in range(1, pack_ref.shape[0]):
        flags = flags + pack_ref[part, 1:2, :]
    flag_col = column(flags, padded)
    lane = lax.broadcasted_iota(I32, (1, padded), 1)
    sub = lax.broadcasted_iota(I32, (padded, 1), 0)
    row = jnp.full((1, padded), -1, I32)
    col = jnp.full((padded, 1), -1, I32)
    for index in range(pos_ref.shape[0]):
        row = jnp.where(lane == index, pos_ref[index], row)
        col = jnp.where(sub == index, pos_ref[index], col)
    return row, col, flags[:, 0:padded] > 0.5, flag_col > 0.5


def key_places(masks, block, span, step):
    place = lax.broadcasted_iota(I32, (1, block), 1)
    if masks is None:
        return place + step * block
    mask = jnp.zeros_like(place)
    for index, value in enumerate(masks):
        mask = jnp.where(place // span == index, value, mask)
    return (lax.axis_index("tile") ^ mask) * span + (place & (span - 1))


def key_rows(place, pos_col, flag_col, offset_ref, span, total):
    rows = branch_rows(place, 0, offset_ref, span, total)
    taken = jnp.where((place == pos_col) & flag_col, 1.0, 0.0)
    taken = jnp.max(taken, axis=0, keepdims=True)
    return as_bf16(rows & (taken < 0.5))


def base_attention_kernel(
    span, total, padded, groups, pos_ref, offset_ref, pack_ref, q_ref, *refs
):
    kv_refs, refs = refs[: len(groups)], refs[len(groups) :]
    kv_ref = kv_refs[0] if len(groups) == 1 else refs[0]
    krows_ref, ml_ref, acc_ref = refs[-3:]
    step = pl.program_id(0)
    rows = q_ref.shape[0]

    masks = None
    if len(groups) > 1:
        masks = sum(groups, ())
        start = 0
        for ref in kv_refs:
            kv_ref[start : start + ref.shape[0], :] = ref[...]
            start += ref.shape[0]
    _, pos_col, _, flag_col = fresh_places(padded, pack_ref, pos_ref)
    place = lax.broadcasted_iota(I32, (rows, 1), 0) + lax.axis_index("tile") * span
    q_rows = stack_heads(as_bf16(branch_rows(place, 1, offset_ref, span, total)), 8)
    block = kv_ref.shape[0]
    if block < total:

        @pl.when(step == 0)
        def _():
            clear_state(ml_ref, acc_ref)

    keys = key_places(masks, kv_ref.shape[0], span, step)
    k_rows = key_rows(keys, pos_col, flag_col, offset_ref, span, total)
    krows_ref[...] = k_rows
    new = attend(stack_heads(q_ref[...], HEAD), q_rows, kv_ref, k_rows)
    if block == total:
        set_stacked(new, ml_ref, acc_ref)
    else:
        add_stacked(new, ml_ref, acc_ref)


def fresh_kernel(
    span, total, pos_ref, offset_ref, pack_ref, q_ref, shares_ref, final_ref, gain_ref,
    wq_ref, wk_ref, wv_ref, ml_ref, acc_ref, rows_ref, *refs,
):
    embed_refs, refs = refs[:4], refs[4:]
    kv_ref, krows_ref, *refs = refs
    outs, refs = refs[:4], refs[4:]
    mine_ref, fresh_s, qf_s, kvf_s, mlf_s, accf_s, mlb_s, att_s = refs
    step = pl.program_id(0)
    rows = q_ref.shape[0]
    padded = fresh_s.shape[0]
    seg = lax.axis_index("seg")
    pos_row, pos_col, flag_row, flag_col = fresh_places(padded, pack_ref, pos_ref)
    f_rows = stack_heads(as_bf16(branch_rows(pos_col, 1, offset_ref, span, total)), 8)

    @pl.when(step == 0)
    def _():
        tiles = shares_ref.shape[0] // 4
        shares = shares_ref[...].astype(F32)
        bias = shares[0:4]
        summed = jnp.sum(shares.reshape(tiles, 4, 16, 128), axis=1)
        pooled = jnp.concatenate([summed[:, row, :] for row in range(DV // 128)], axis=1)
        summary = layer_norm(pooled, final_ref[...].reshape(1, DV)).astype(BF16)
        fresh_s[...] = jnp.zeros_like(fresh_s)
        pieces = [dot_nt(summary, ref[:, 0:DV]) for ref in embed_refs]
        for part in range(4):
            piece = pieces[0]
            for mask in range(1, 4):
                piece = jnp.where((seg ^ part) == mask, pieces[mask], piece)
            own = bias[part]
            own = own[12:14] + own[14:16]
            own = jnp.concatenate([own[0:1], own[1:2, 0:64]], axis=1)
            piece = (piece + own).astype(BF16).astype(F32)
            fresh_s[0:tiles, part * 192 : (part + 1) * 192] = piece
        normed = layer_norm(fresh_s[...], gain_ref[...].reshape(1, DS)).astype(BF16)
        project(normed, wq_ref, wk_ref, wv_ref, qf_s, kvf_s)
        clear_state(mlf_s, accf_s)

    qf = stack_heads(qf_s[...], HEAD)
    new = attend(qf, f_rows, kv_ref, krows_ref[...])
    if kv_ref.shape[0] == total:
        set_stacked(new, mlf_s, accf_s)
    else:
        add_stacked(new, mlf_s, accf_s)

    @pl.when(step == pl.num_programs(0) - 1)
    def _():
        first = lax.axis_index("tile") * span
        place = lax.broadcasted_iota(I32, (rows, 1), 0) + first
        q_rows = stack_heads(as_bf16(branch_rows(place, 1, offset_ref, span, total)), 8)
        k_rows = as_bf16(branch_rows(pos_row, 0, offset_ref, span, total) & flag_row)
        mlb_s[...] = ml_ref[...]
        att_s[...] = acc_ref[...]
        add_stacked(attend(stack_heads(q_ref[...], HEAD), q_rows, kvf_s, k_rows), mlb_s, att_s)
        base = finish(mlb_s, att_s)
        add_stacked(attend(qf, f_rows, kvf_s, k_rows), mlf_s, accf_s)
        fresh = finish(mlf_s, accf_s)
        chosen = as_bf16((place == pos_row) & flag_row)
        hit = jnp.sum(chosen.astype(F32), axis=1, keepdims=True) > 0.5
        att_s[...] = jnp.where(hit, dot(chosen, fresh.astype(BF16)), base)
        count = rows // 4
        for mask in range(4):
            start = pl.multiple_of((seg ^ mask) * count, count)
            outs[mask][...] = att_s[pl.ds(start, count), :].astype(BF16)
        start = pl.multiple_of(seg * count, count)
        place = lax.broadcasted_iota(I32, (count, 1), 0) + first + start
        chosen = as_bf16((place == pos_row) & flag_row)
        hit = jnp.sum(chosen.astype(F32), axis=1, keepdims=True) > 0.5
        placed = dot(chosen, fresh_s[...].astype(BF16))
        old = rows_ref[pl.ds(start, count), :].astype(F32)
        mine_ref[...] = jnp.where(hit, placed, old)


def out_kernel(mine_ref, *refs):
    out_ref = refs[8]
    total = mine_ref[...]
    for mask in range(4):
        att, weight = refs[mask][...], refs[4 + mask][...]
        total = total + dot(att[:, 128:256], weight[0:128])
        total = total + dot(att[:, 64:128], weight[128:192])
    out_ref[...] = total.astype(BF16)


def trade(block, axis, mask):
    count = lax.axis_size(axis)
    return lax.ppermute(block, axis, [(i, i ^ mask) for i in range(count)])


GROUPS = ((0,), (2, 4, 6), (1,), (3, 5, 7))


def together(*values):
    return lax.optimization_barrier(values)


def shards(
    patches, vit_norm_gain, vit_query, vit_key, vit_value, vit_out, layer_scale, final_gain,
    embed_proj, embed_bias, slide_pos, cached, kept, mask_token, slide_gain, slide_query,
    slide_key, slide_value, slide_out, offsets,
):
    tiles = lax.axis_size("tile")
    segs = lax.axis_size("seg")
    devices = tiles * segs
    span = cached.shape[0]
    total = span * tiles
    cut, local_cols = vit_query.shape
    fresh = slide_pos.shape[0]
    padded = max(16, fresh)
    small = tiles == 8
    call = pl.pallas_call
    sds = jax.ShapeDtypeStruct
    weights = (slide_query.T, slide_key.T, slide_value.T)
    embed = embed_proj.T

    pack = call(
        functools.partial(class_kernel, fresh),
        out_shape=sds((tiles, 8, 256), F32),
        grid=(1,),
        in_specs=[pl.BlockSpec((1, 16, DV), lambda i: (0, 0, 0)), VMEM, SMEM, VMEM],
        out_specs=VMEM,
        compiler_params=params(60),
        name="class_row",
    )(patches, vit_norm_gain, slide_pos, kept)
    pack, value, cached = together(pack, vit_value, cached)
    pack = lax.all_to_all(pack, "tile", 0, 0, tiled=True)
    base_rows, q_base, kv_base, joined = call(
        base_kernel,
        out_shape=(
            sds((span, DS), BF16), sds((span, 256), BF16), sds((span, 384), BF16),
            sds((192, DV + DS), BF16),
        ),
        in_specs=[VMEM] * 9,
        out_specs=(VMEM,) * 4,
        compiler_params=params(60),
        name="base_rows",
    )(cached, kept, mask_token, slide_gain, *weights, embed, slide_out)
    joined_x = trade(joined, "seg", 2)
    if small:
        value_z = jnp.concatenate([trade(value, "tile", mask) for mask in GROUPS[1]], axis=0)
        value_y = trade(value, "tile", 1)
        kv_y = trade(kv_base, "tile", 1)

    due = [value_y] if small else []
    part_shape = (tiles, fresh, local_cols) if small else (fresh, local_cols)
    part = call(
        functools.partial(query_kernel, cut),
        out_shape=sds(part_shape, F32),
        in_specs=[VMEM] * 2 + [ANY] * len(due),
        out_specs=VMEM,
        compiler_params=params(8 if small else 16),
        name="query_share",
    )(pack, vit_query, *due)
    if small:
        part, value_z, kv_own = together(part, value_z, kv_base)
        part = lax.all_to_all(part, "tile", 0, 0, tiled=True)
    else:
        part = lax.psum(part, "tile")
    normed = call(
        token_kernel,
        out_shape=sds(patches.shape[1:], BF16),
        in_specs=[VMEM] * 2,
        out_specs=VMEM,
        compiler_params=params(12),
        name="token_norm",
    )(patches, vit_norm_gain)
    joined, joined_x = together(joined, joined_x)
    joined_all = [joined, trade(joined, "seg", 1), joined_x, trade(joined_x, "seg", 1)]
    if small:
        wv_all = [value, value_z, value_y, trade(value_z, "tile", 1)]
        kv_z = jnp.concatenate([trade(kv_own, "tile", mask) for mask in GROUPS[1]], axis=0)
    else:
        wv_all = [lax.all_gather(value, "tile", axis=0, tiled=True)]

    due = [kv_y, wv_all[3]] if small else []
    folded = call(
        fold_kernel,
        out_shape=sds((fresh, 8, round_up(cut, 128)), F32),
        in_specs=[VMEM] * 2 + [ANY] * len(due),
        out_specs=VMEM,
        compiler_params=params(8 if small else 16),
        name="fold_key",
    )(part, vit_key, *due)
    if small:
        groups = GROUPS
    else:
        kv_all = [lax.all_gather(kv_base, "tile", axis=0, tiled=True)]
        groups = (None,)
    folded = lax.all_to_all(folded, "tile", 0, 0, tiled=True)
    if small:
        kv_z = call(
            gate_kernel,
            out_shape=sds(kv_z.shape, kv_z.dtype),
            in_specs=[ANY] * 2,
            out_specs=ANY,
            input_output_aliases={0: 0},
            compiler_params=params(8),
            name="third_over",
        )(kv_z, folded)
        kv_all = [kv_own, kv_z, kv_y, trade(kv_z, "tile", 1)]
    sent = call(
        functools.partial(tile_kernel, cut),
        out_shape=sds((devices, 16, 128), BF16),
        grid=(1,),
        in_specs=[pl.BlockSpec((1, 16, DV), lambda i: (0, 0, 0))] + [VMEM] * (5 + len(wv_all)),
        out_specs=VMEM,
        scratch_shapes=[
            pltpu.VMEM((8, DV), F32), pltpu.VMEM((tiles, 8, round_up(cut, 128)), F32),
            pltpu.VMEM((16, 128), F32),
        ],
        compiler_params=params(60),
        name="tile_attention",
    )(patches, normed, folded, layer_scale, embed_bias, vit_out, *wv_all)
    shares = lax.all_to_all(sent, ("tile", "seg"), 0, 0, tiled=True)
    block = min(total, 2048)
    steps = total // block
    kv_spec = pl.BlockSpec((block, 384), lambda i: (i, 0))
    krows_spec = pl.BlockSpec((24, block), lambda i: (0, i))
    kv_shape = [sds((total, 384), BF16)] if small else []
    *kv_sorted, krows, ml, acc = call(
        functools.partial(base_attention_kernel, span, total, padded, groups),
        out_shape=(
            *kv_shape, sds((24, total), BF16), sds((span, 128), F32), sds((span, 256), F32),
        ),
        grid=(steps,),
        in_specs=[SMEM, SMEM, VMEM, VMEM] + ([VMEM] * 4 if small else [kv_spec]),
        out_specs=(*([kv_spec] if small else []), krows_spec, VMEM, VMEM),
        compiler_params=params(60),
        name="base_attention",
    )(slide_pos, offsets, pack, q_base, *kv_all)
    kv_sorted = kv_sorted[0] if small else kv_all[0]

    count = span // segs
    outs = call(
        functools.partial(fresh_kernel, span, total),
        out_shape=(sds((count, 256), BF16),) * 4 + (sds((count, DS), F32),),
        grid=(steps,),
        in_specs=[SMEM] * 2 + [VMEM] * 9 + [VMEM] * 2
        + [pl.BlockSpec((192, DV), lambda i: (0, 0))] * 4 + [kv_spec, krows_spec],
        out_specs=(VMEM,) * 5,
        scratch_shapes=[
            pltpu.VMEM((padded, DS), F32),
            pltpu.VMEM((padded, 256), BF16),
            pltpu.VMEM((padded, 384), BF16),
            pltpu.VMEM((padded, 128), F32),
            pltpu.VMEM((padded, 256), F32),
            pltpu.VMEM((span, 128), F32),
            pltpu.VMEM((span, 256), F32),
        ],
        compiler_params=params(60),
        name="fresh_attention",
    )(
        slide_pos, offsets, pack, q_base, shares, final_gain, slide_gain, *weights, ml, acc,
        base_rows, *joined_all, kv_sorted, krows,
    )
    swapped = [outs[0]] + [trade(outs[mask], "seg", mask) for mask in range(1, 4)]
    return call(
        out_kernel,
        out_shape=sds((count, DS), BF16),
        grid=(1,),
        in_specs=[VMEM] * 5 + [pl.BlockSpec((192, DS), lambda i: (0, DV // DS))] * 4,
        out_specs=VMEM,
        compiler_params=params(60),
        name="slide_next",
    )(outs[4], *swapped, *joined_all)


def solution(mesh):
    return jax.shard_map(
        shards,
        mesh=mesh,
        in_specs=(
            P("tile", None, None), P(), P("tile", "seg"), P("tile", "seg"), P("tile", "seg"),
            P("seg", None), P(), P(), P(None, "seg"), P("seg"), P(), P("tile", None), P("tile"),
            P(), P(), P(None, "seg"), P(None, "seg"), P(None, "seg"), P("seg", None), P(),
        ),
        out_specs=P(("tile", "seg"), None),
        check_vma=False,
    )
```
